32 devices in a mesh: dp: 8 (over y, x, core), shard: 4 (over z).
Axes of the slice: x: 2, y: 2, z: 4, core: 2. Of those that a mesh axis runs over, the one named last changes fastest.
Arguments:
- features: bfloat16 [65536, 2048], P(('dp', 'shard')), may hold values from -6 to 6
- neighbors: int32 [65536, 128], P(('dp', 'shard')), may hold values from -1 to 1023, as said below
- weight: bfloat16 [2048, 2048], P(('dp', 'shard')), may hold values from -0.125 to 0.125
- bias_terms: bfloat16 [2048], P(('dp', 'shard')), may hold values from -1.796875 to 1.796875
- grad_out: bfloat16 [65536, 2048], P(('dp', 'shard')), may hold values from -6 to 6
Outputs:
- activations: bfloat16 [65536, 2048], P(('dp', 'shard'))
- grad_features: float32 [65536, 2048], P(('dp', 'shard'))
- grad_weight: float32 [2048, 2048], P(('dp', 'shard'))
- grad_bias: float32 [2048], P(('dp', 'shard'))
The draws below stay inside these ranges and needn't reach their ends.
Inputs may be any that keep to these rules, and one draw needn't show every extreme that they name: `neighbors`: each row lists neighbours of its node as indices within its cluster (clusters are aligned blocks of 1024 rows): used slots first, then -1 pads. An index may repeat; each slot counts as one edge. Every row has at least one neighbour, and the first row of every cluster uses all 128 slots.
All inputs are finite; a program needn't handle non-finite values.
Results may differ from the reference program's by a relative error of at most 0.0057.
Values may be sent and summed in bfloat16 or wider, within the bound.
A program may use at most 192 MiB of HBM per device.

```python
import jax
import jax.numpy as jnp
from jax import lax

WIDTH = 2048
CLUSTER = 1024
SLOTS = 128
NODES = 65536


def draw_neighbors(key, part):
    first_key, second_key, third_key = jax.random.split(jax.random.fold_in(key, 17), 3)
    tiers = jax.random.randint(first_key, (NODES,), 0, 8)
    limits = jnp.maximum(1, jnp.right_shift(jnp.full((NODES,), SLOTS, jnp.int32), tiers))
    degree = jax.random.randint(second_key, (NODES,), 1, limits + 1)
    rows = lax.broadcasted_iota(jnp.int32, (NODES,), 0)
    degree = jnp.where(rows % CLUSTER == 0, SLOTS, degree)
    chosen = jax.random.randint(third_key, (NODES, SLOTS), 0, CLUSTER)
    slot_ids = lax.broadcasted_iota(jnp.int32, (NODES, SLOTS), 1)
    return jnp.where(slot_ids < degree[:, None], chosen, -1).astype(jnp.int32)


def block_scale(own_key, dims, cuts, smallest, largest):
    factor_of, own = 1.0, jax.random.fold_in(own_key, 6)
    for position, parts in cuts:
        draws = jnp.exp(jax.random.uniform(jax.random.fold_in(own, position), (parts,), jnp.float32, smallest / len(cuts), largest / len(cuts)))
        factor_of = factor_of * jnp.repeat(draws, dims[position] // parts).reshape([-1 if axis == position else 1 for axis in range(len(dims))])
    return factor_of


def gaussian(own_key, shape, deviation, reach, shards=(), held_as=jnp.bfloat16):
    array = deviation * jax.random.normal(own_key, shape, jnp.float32)
    if shards:
        array = array * block_scale(own_key, shape, shards, -0.22, 0.18)
    return jnp.clip(array, -reach, reach).astype(held_as)


def setup_inputs(seed: int = 0) -> dict:
    arg_keys = jax.random.split(jax.random.key(seed), 6)
    features = gaussian(arg_keys[0], (NODES, WIDTH), 1.0, 6.0, ((0, 32),))
    neighbors = draw_neighbors(jax.random.fold_in(arg_keys[5], 71), 0)
    weight = gaussian(arg_keys[2], (WIDTH, WIDTH), WIDTH ** -0.5, 0.125, ((0, 32),))
    bias_terms = gaussian(arg_keys[3], (WIDTH,), 0.3, 1.796875, ((0, 32),))
    grad_out = gaussian(arg_keys[4], (NODES, WIDTH), 1.0, 6.0, ((0, 32),))
    return dict(features=features, neighbors=neighbors, weight=weight, bias_terms=bias_terms, grad_out=grad_out)


@jax.custom_vjp
def low(v):
    return lax.optimization_barrier(v.astype(jnp.bfloat16)).astype(jnp.float32)

@jax.custom_vjp
def low_back(v):
    return v

def low_keep(v):
    return (low(v), None)

def low_pass(kept, grad):
    return (grad,)

def back_keep(v):
    return (v, None)

def back_low(kept, grad):
    return (low(grad),)
low.defvjp(low_keep, low_pass)
low_back.defvjp(back_keep, back_low)

def adjacency(neighbor_rows):
    node_total = neighbor_rows.shape[0]
    slot_total = neighbor_rows.shape[1]
    columns = lax.broadcasted_iota(jnp.int32, (1, 1, node_total), 2)
    groups = jnp.transpose(neighbor_rows.reshape(node_total, slot_total // 8, 8), (1, 0, 2))

    def add_group(running, group_ids):
        matches = lax.optimization_barrier(jnp.sum((group_ids[:, :, None] == columns).astype(jnp.float32), axis=1))
        return (running + matches, None)
    running, unused = lax.scan(add_group, jnp.zeros((node_total, node_total), jnp.float32), groups)
    return running

def cluster_mix(paired):
    block_rows, neighbor_rows = paired
    return jnp.dot(adjacency(neighbor_rows), block_rows, precision=lax.Precision.HIGHEST)

def reference(features, neighbors, weight, bias_terms, grad_out):
    node_count = features.shape[0]
    cluster_count = node_count // CLUSTER
    degree = lax.optimization_barrier(jnp.sum((neighbors >= 0).astype(jnp.float32), axis=1, keepdims=True))
    factor = 1.0 / (degree + 1.0)
    neighbor_blocks = neighbors.reshape(cluster_count, CLUSTER, SLOTS)

    def forward(feature_rows, weight_rows, bias_rows):
        summed = lax.map(jax.checkpoint(cluster_mix), (feature_rows.reshape(cluster_count, CLUSTER, WIDTH), neighbor_blocks))
        summed = summed.reshape(node_count, WIDTH)
        mixed_rows = low(factor * low_back(2.0 * feature_rows + summed))
        linear = low_back(jnp.dot(mixed_rows, weight_rows, precision=lax.Precision.HIGHEST) + bias_rows)
        return jax.nn.gelu(linear, approximate=True)
    output, pullback = jax.vjp(forward, features.astype(jnp.float32), weight.astype(jnp.float32), bias_terms.astype(jnp.float32))
    grad_features, grad_weight, grad_bias = pullback(grad_out.astype(jnp.float32))
    return (output.astype(jnp.bfloat16), grad_features, grad_weight, grad_bias)
```

```python
import jax
import jax.numpy as jnp
from jax import lax
from jax.experimental import pallas as pl
from jax.experimental.pallas import tpu as pltpu
from jax.sharding import PartitionSpec as P

F32, BF16, I32 = jnp.float32, jnp.bfloat16, jnp.int32
MESH = pl.DeviceIdType.MESH
CLUSTER = 1024
SLOTS = 128
UNROLL = 16
PC = 512
HC = 256
ALPHA = 0.7978845608028654
BETA = ALPHA * 0.044715
NN = (((1,), (0,)), ((), ()))
TN = (((0,), (0,)), ((), ()))
NT = (((1,), (1,)), ((), ()))
ALL = slice(None)

GATHER = ("zxy", "zyx", "zxy", "zyx", "xzy", "yzx", "zxy", "zyx")
SCATTER = ("yxz", "xyz", "yzx", "xzy", "yxz", "xyz", "yxz", "xyz")
COUNT_EVENTS = (
    (3, "second", 0),
    (3, "first", 1),
    (5, "third", 0),
    (6, "second", 1),
    (6, "second", 2),
    (8, "third", 1),
    (8, "first", 3),
    (9, "pass", 0),
    (12, "third", 2),
    (12, "second", 3),
    (13, "pass", 1),
    (15, "third", 3),
)
MIX_EVENTS = ((4, "pass", 2),)
SUM_EVENTS = ((4, 1, 0), (6, 1, 1), (7, 2, 0))
BACK_EVENTS = (
    (0, 3, 0),
    (1, 2, 1),
    (2, 1, 2),
    (3, 3, 1),
    (4, 2, 2),
    (5, 1, 3),
    (6, 3, 2),
    (7, 2, 3),
)


def dot(a, b, dims):
    return lax.dot_general(a, b, dims, preferred_element_type=F32)


class Place:
    def __init__(self, dp_size, shard_size):
        dp, self.z = lax.axis_index("dp"), lax.axis_index("shard")
        self.dp = dp
        self.c, self.x, self.y = dp % 2, (dp // 2) % 2, dp // 4
        self.size = {"c": 2, "x": 2, "y": dp_size // 4, "z": shard_size}

    def at(self, dim):
        return {"c": self.c, "x": self.x, "y": self.y, "z": self.z}[dim]

    def shifted(self, dim, offset):
        size = self.size[dim]
        return lax.rem(self.at(dim) + (offset + size), size)

    def peer(self, dim, offset):
        other = self.shifted(dim, offset)
        if dim == "z":
            return (self.dp, other)
        step = {"c": 1, "x": 2, "y": 4}[dim]
        return (self.dp + step * (other - self.at(dim)), self.z)

    def offsets(self, dim):
        return range(1, self.size[dim])


class Sems:
    def __init__(self):
        self.index = {}

    def __getitem__(self, name):
        return self.index.setdefault(name, len(self.index))


def sem_names(sizes):
    sems = Sems()
    for t in list(range(len(GATHER))) + ["bias"]:
        path = GATHER[0] if t == "bias" else GATHER[t]
        for k in range(3):
            for o in range(1, sizes[path[k]]):
                sems["gather", t, k, o]
        sems["core", t, 0]
        for o in range(1, sizes[path[2]]):
            sems["core", t, o]
    for t in list(range(len(SCATTER))) + ["bias"]:
        path = SCATTER[0] if t == "bias" else SCATTER[t]
        for k in range(3):
            for o in range(1, sizes[path[k]]):
                for h in range(2 if k == 0 and path[0] == "x" else 1):
                    sems["scatter", t, k, o, h]
    sems["swap", "bias"]
    for s in range(len(SCATTER)):
        sems["swap", s]
    return sems


def linkable(rows):
    return rows % 16 == 0


def make_kernel(dp_size, shard_size, rows, width, nodes):
    sizes = {"c": 2, "x": 2, "y": dp_size // 4, "z": shard_size}
    Y, X, S, R = sizes["y"], 2, shard_size, rows
    SR = S * R
    n_dev = dp_size * shard_size
    panels = width // PC
    half_rows = width // 2
    clusters = nodes // CLUSTER
    sems = sem_names(sizes)
    n_sems = len(sems.index)
    chunks = nodes // 128
    TM = 512
    tiles = (nodes // TM) * panels
    per_panel = nodes // TM
    FW = width // Y

    def stage_shape(path, k):
        n = sizes[path[k]] - 1
        left = path[k + 1 :]
        lead = tuple(sizes[d] for d in "yx" if d in left)
        return (n,) + lead, ("z" in left)

    def stage_shapes():
        out = []
        for t in range(len(SCATTER)):
            for k in range(3):
                lead, z = stage_shape(SCATTER[t], k)
                out.append(pltpu.VMEM(lead + (SR if z else R, HC), BF16))
        for k in range(3):
            lead, z = stage_shape(SCATTER[0], k)
            out.append(pltpu.VMEM(lead + (S if z else 1, 8, 128), F32))
        return out

    n_stage = 3 * (len(SCATTER) + 1)
    linked = linkable(rows)

    def kernel(
        f_hbm, n_hbm, w_hbm, b_hbm, g_hbm,
        act_hbm, sp_hbm, a_hbm, gw_hbm, gb_hbm,
        fg, mixed, wg, a2t, fac, bt, brow, gbacc, cr, crb, ptb, gws, gbs, *rest,
    ):
        stage = rest[:n_stage]
        ssem, rsem, lsem = rest[n_stage:]
        me = Place(dp_size, shard_size)
        c, x, y, z = me.c, me.x, me.y, me.z
        started = []

        def remote(name, src, dst, device):
            i = sems[name]
            return pltpu.make_async_remote_copy(
                src_ref=src, dst_ref=dst, send_sem=ssem.at[i], recv_sem=rsem.at[i],
                device_id=device, device_id_type=MESH,
            )

        def send(name, make):
            remote(name, *make()).start()
            started.append((name, make))

        def arrived(name, ref):
            remote(name, ref, ref, me.peer("c", 1)).wait_recv()

        def view(t, core, **at):
            ys, xs = at.get("y", ALL), at.get("x", ALL)
            if t == "bias":
                zs = pl.ds(at["z"], 1) if "z" in at else ALL
                return bt.at[ys, xs, core, zs]
            zs = pl.ds(pl.multiple_of(at["z"] * R, R), R) if "z" in at else ALL
            return wg.at[t // 2, ys, xs, core, zs, pl.ds(t % 2 * HC, HC)]

        own = {"x": x, "y": y, "z": z}

        def fixed(dims):
            return {d: own[d] for d in dims}

        def gather_path(t):
            return GATHER[0] if t == "bias" else GATHER[t]

        def gather_first(t):
            path = gather_path(t)

            def make(o):
                if t == "bias":
                    return b_hbm, bt.at[y, x, c, z], me.peer(path[0], o)
                src = w_hbm.at[:, pl.ds(t * HC, HC)]
                return src, view(t, c, **fixed("xyz")), me.peer(path[0], o)

            for o in me.offsets(path[0]):
                send(("gather", t, 0, o), lambda o=o: make(o))

        def gather_wait(t, k):
            path = gather_path(t)
            for o in me.offsets(path[k]):
                at = fixed(path[k:])
                at[path[k]] = me.shifted(path[k], -o)
                arrived(("gather", t, k, o), view(t, c, **at))

        def gather_send(t, k):
            path = gather_path(t)

            def make(o):
                ref = view(t, c, **fixed(path[k:]))
                return ref, ref, me.peer(path[k], o)

            for o in me.offsets(path[k]):
                send(("gather", t, k, o), lambda o=o: make(o))

        def core_send(t, late):
            path = gather_path(t)

            def make(o):
                at = {path[2]: me.shifted(path[2], -o)} if o else fixed(path[2:])
                ref = view(t, c, **at)
                return ref, ref, me.peer("c", 1)

            for o in me.offsets(path[2]) if late else (0,):
                send(("core", t, o), lambda o=o: make(o))

        def core_wait(t):
            path = gather_path(t)
            arrived(("core", t, 0), view(t, 1 - c, **fixed(path[2:])))
            for o in me.offsets(path[2]):
                arrived(
                    ("core", t, o),
                    view(t, 1 - c, **{path[2]: me.shifted(path[2], -o)}),
                )

        def slices(panel):
            return (2 * panel, 2 * panel + 1) + (("bias",) if panel == 0 else ())

        def own_block(j):
            if not linked:
                return pltpu.make_async_copy(
                    w_hbm.at[:, :, :, :, pl.ds(j * PC, PC)], wg.at[j], lsem.at[8 + j]
                )
            return pltpu.make_async_copy(
                w_hbm.at[:, pl.ds(j * PC, PC)],
                wg.at[j, y, x, c, pl.ds(pl.multiple_of(z * R, R), R), :],
                lsem.at[8 + j],
            )

        def own_bias():
            if not linked:
                return pltpu.make_async_copy(b_hbm, brow, lsem.at[8 + panels])
            return pltpu.make_async_copy(b_hbm, bt.at[y, x, c, z], lsem.at[8 + panels])

        def gather_event(kind, panel):
            if not linked:
                if kind == "ready":
                    own_block(panel).wait()
                if kind == "ready" and panel == 0:
                    own_bias().wait()
            elif kind == "first":
                for t in slices(panel):
                    gather_first(t)
            elif kind == "second":
                for t in slices(panel):
                    gather_wait(t, 0)
                own_block(panel).wait()
                if panel == 0:
                    own_bias().wait()
                for t in slices(panel):
                    gather_send(t, 1)
            elif kind == "third":
                for t in slices(panel):
                    gather_wait(t, 1)
                for t in slices(panel):
                    gather_send(t, 2)
                for t in slices(panel):
                    core_send(t, False)
            elif kind == "pass":
                for t in slices(panel):
                    gather_wait(t, 2)
                for t in slices(panel):
                    core_send(t, True)
            elif kind == "ready":
                for t in slices(panel):
                    core_wait(t)

        load_n = lambda ref: pltpu.make_async_copy(n_hbm, ref, lsem.at[9 + panels])
        load_f = pltpu.make_async_copy(f_hbm, fg, lsem.at[10 + panels])

        def count_phase(nb, lo_s, wa_s, wb_s):
            load_n(nb).start()
            peers = [me.peer(d, o) for d in "cxyz" for o in me.offsets(d) if linked]
            for p in peers:
                pl.semaphore_signal(
                    pltpu.get_barrier_semaphore(), inc=1,
                    device_id=p, device_id_type=MESH,
                )
            for j in range(panels):
                own_block(j).start()
            own_bias().start()
            if linked:
                pl.semaphore_wait(pltpu.get_barrier_semaphore(), len(peers))
            gather_event("first", 0)
            gather_event("first", 2)
            load_f.start()
            load_n(nb).wait()

            @pl.loop(0, chunks)
            def _(q):
                r = pl.ds(pl.multiple_of(q * 128, 128), 128)
                ids = nb[r, :]
                degree = jnp.sum((ids >= 0).astype(F32), axis=1, keepdims=True)
                fac[r, :] = jnp.broadcast_to(1.0 / (degree + 1.0), (128, 128))
                ids = ids.T
                group = ids >> 7
                digit = jnp.left_shift(jnp.ones_like(ids), (group & 3) * 8)
                lo_s[:, r] = ids & 127
                wa_s[:, r] = jnp.where((group >= 0) & (group < 4), digit, 0)
                wb_s[:, r] = jnp.where(group >= 4, digit, 0)

            lane = lax.broadcasted_iota(I32, (128, 128), 0)
            twice = jnp.where(
                lane == lax.broadcasted_iota(I32, (128, 128), 1), 2.0, 0.0
            )

            @pl.loop(0, chunks)
            def _(q):
                col = pl.ds(pl.multiple_of(q * 128, 128), 128)

                def step(s, carry):
                    a, b = carry
                    rows_ = pl.ds(pl.multiple_of(s * UNROLL, UNROLL), UNROLL)
                    lo, wa, wb = lo_s[rows_, col], wa_s[rows_, col], wb_s[rows_, col]
                    for k in range(UNROLL):
                        hit = lo[k : k + 1] == lane
                        a = a + jnp.where(hit, wa[k : k + 1], 0)
                        b = b + jnp.where(hit, wb[k : k + 1], 0)
                    return a, b

                zero = jnp.zeros((128, 128), I32)
                a, b = lax.fori_loop(0, SLOTS // UNROLL, step, (zero, zero))
                cl, place = q // 8, q % 8
                to = pl.ds(pl.multiple_of(place * 128, 128), 128)
                for h in range(8):
                    count = ((a if h < 4 else b) >> (8 * (h % 4))) & 255
                    count = count.astype(F32) + jnp.where(place == h, twice, 0.0)
                    a2t[cl, pl.ds(h * 128, 128), to] = count.astype(BF16)
                for at, kind, panel in COUNT_EVENTS:
                    pl.when(q == at)(lambda k=kind, p=panel: gather_event(k, p))

        pl.run_scoped(
            count_phase,
            pltpu.VMEM((nodes, SLOTS), I32),
            *[pltpu.VMEM((SLOTS, nodes), I32)] * 3,
        )
        store_a = pltpu.make_async_copy(a2t, a_hbm, lsem.at[11 + panels])
        store_a.start()
        load_f.wait()

        @pl.loop(0, clusters * 4)
        def _(s):
            cl, i, j = s // 4, (s // 2) % 2, s % 2
            r = pl.ds(pl.multiple_of(cl * CLUSTER + i * 512, 512), 512)
            k = pl.ds(pl.multiple_of(cl * CLUSTER, CLUSTER), CLUSTER)
            col = pl.ds(pl.multiple_of(j * half_rows, half_rows), half_rows)
            links = a2t[cl, :, pl.ds(pl.multiple_of(i * 512, 512), 512)]
            total = dot(links, fg[k, col], TN)
            scale = jnp.concatenate([fac[r, :]] * (half_rows // 128), axis=1)
            mixed[r, col] = (scale * total).astype(BF16)
            for at, kind, panel in MIX_EVENTS:
                pl.when(s == at)(lambda k=kind, p=panel: gather_event(k, p))

        def linear_phase(acc_a, acc_b, go, ac):
            def where(n):
                return n // per_panel, n % per_panel

            def block(hbm, n):
                j, i = where(n)
                return hbm.at[
                    pl.ds(pl.multiple_of(i * TM, TM), TM),
                    pl.ds(pl.multiple_of(j * PC, PC), PC),
                ]

            def load_g(n, slot):
                return pltpu.make_async_copy(
                    block(g_hbm, n), go.at[slot], lsem.at[slot]
                )

            def store_act(n, slot):
                return pltpu.make_async_copy(
                    ac.at[slot], block(act_hbm, n), lsem.at[4 + slot]
                )

            def product(n):
                j, i = where(n)
                panel = wg[j].reshape(width, PC)
                return dot(mixed[pl.ds(pl.multiple_of(i * TM, TM), TM), :], panel, NN)

            def finish(acc, n, slot):
                j, i = where(n)
                r = pl.ds(pl.multiple_of(i * TM, TM), TM)
                col = pl.ds(pl.multiple_of(j * PC, PC), PC)
                v = acc[...] + brow[0:1, col]
                u = v * v
                h = 0.5 + 0.5 * jnp.tanh(v * (ALPHA + BETA * u))
                a = v * h
                d = h + (a * (1.0 - h)) * (2 * ALPHA + (6 * BETA) * u)
                g = go[slot].astype(F32) * d
                ac[slot] = a.astype(BF16)
                fg[r, col] = g.astype(BF16)
                gbacc[:, col] += jnp.sum(g.reshape(TM // 8, 8, PC), axis=0)

            gather_event("ready", 0)
            p = 128 // R
            for k in range(width // 128 if linked else 0):
                tile = jnp.zeros((8, 128), F32)
                for d in range(k * p, (k + 1) * p):
                    tile = tile + bt[d // (X * 2 * S), d // (2 * S) % X, d // S % 2, d % S]
                brow[:, pl.ds(k * 128, 128)] = tile
            gbacc[...] = jnp.zeros_like(gbacc)
            for n in range(2):
                load_g(n, n).start()
            acc_a[...] = product(0)

            def pair(t, last):
                n = 2 * t
                slot = t % 2 * 2
                load_g(n, slot).wait()
                load_g(n + 1, slot + 1).wait()
                if not last:
                    other = 2 - slot
                    load_g(n + 2, other).start()
                    load_g(n + 3, other + 1).start()

                @pl.when(jnp.asarray(t >= 2))
                def _():
                    store_act(n - 4, slot).wait()
                    store_act(n - 3, slot + 1).wait()

                acc_b[...] = product(n + 1)
                finish(acc_a, n, slot)
                if not last:
                    acc_a[...] = product(n + 2)
                finish(acc_b, n + 1, slot + 1)
                store_act(n, slot).start()
                store_act(n + 1, slot + 1).start()

            @pl.loop(0, tiles // 2 - 1)
            def _(t):
                for j in range(1, panels):

                    @pl.when(t == (per_panel // 2) * j - 1)
                    def _():
                        if j == 1:
                            gather_event("pass", 3)
                        gather_event("ready", j)

                pair(t, False)

            last = tiles // 2 - 1
            pair(last, True)
            for n in range(tiles - 4, tiles):
                store_act(n, n % 4).wait()

        pl.run_scoped(
            linear_phase,
            *[pltpu.VMEM((TM, PC), F32)] * 2,
            *[pltpu.VMEM((4, TM, PC), BF16)] * 2,
        )
        store_a.wait()

        def back_phase(pt, sp):
            half_y = Y // 2
            y_half = y // half_y

            def half_of(hh):
                if isinstance(hh, int):
                    return y_half if hh else 1 - y_half
                return jnp.where(hh == 0, 1 - y_half, y_half)

            def part(t, core, **at):
                ys, xs = at.get("y", ALL), at.get("x", ALL)
                if t == "bias":
                    zs = pl.ds(at["z"], 1) if "z" in at else ALL
                    return ptb.at[ys, xs, core, zs]
                zs = pl.ds(pl.multiple_of(at["z"] * R, R), R) if "z" in at else ALL
                return pt.at[t // 2, ys, xs, core, zs, pl.ds(t % 2 * HC, HC)]

            def scatter_path(t):
                return SCATTER[0] if t == "bias" else SCATTER[t]

            def landing(t, k):
                return stage[(len(SCATTER) if t == "bias" else t) * 3 + k]

            def scatter_send(t, k, h=None):
                path = scatter_path(t)

                def make(o):
                    at = fixed(path[:k])
                    at[path[k]] = me.shifted(path[k], o)
                    dst = landing(t, k).at[o - 1]
                    if h is not None:
                        ys = pl.ds(half_of(h) * half_y, half_y)
                        at["y"] = ys
                        dst = dst.at[ys]
                    return part(t, c, **at), dst, me.peer(path[k], o)

                for o in me.offsets(path[k]):
                    send(("scatter", t, k, o, h or 0), lambda o=o: make(o))

            def scatter_wait(t, k):
                path = scatter_path(t)
                for o in me.offsets(path[k]):
                    ref = landing(t, k).at[o - 1]
                    if t != "bias" and k == 0 and path[0] == "x":
                        for i in range(2):
                            ys = pl.ds(half_of(i) * half_y, half_y)
                            arrived(("scatter", t, k, o, i), ref.at[ys])
                    else:
                        arrived(("scatter", t, k, o, 0), ref)

            def scatter_add(t, k):
                path = scatter_path(t)
                mine = part(t, c, **fixed(path[: k + 1]))
                total = mine[...].astype(F32)
                for o in me.offsets(path[k]):
                    total = total + landing(t, k)[o - 1].astype(F32)
                if k < 2:
                    mine[...] = total.astype(mine.dtype)
                elif t == "bias":
                    gbs[...] = total.reshape(8, 128)
                else:
                    gws[:, pl.ds(t * HC, HC)] = total

            def swap(s):
                j, hh = s // 2, s % 2
                ys = pl.ds(half_of(hh) * half_y, half_y)
                i = sems["swap", 0] + s
                return pltpu.make_async_remote_copy(
                    src_ref=pt.at[j, ys, :, 1 - c], dst_ref=cr.at[j, ys],
                    send_sem=ssem.at[i], recv_sem=rsem.at[i],
                    device_id=me.peer("c", 1), device_id_type=MESH,
                )

            def core_sum(s):
                j, hh = s // 2, s % 2
                swap(s).wait_recv()
                ys = pl.ds(half_of(hh) * half_y, half_y)
                mine = pt.at[j, ys, :, c]
                mine[...] = (mine[...].astype(F32) + cr[j, ys].astype(F32)).astype(BF16)
                for t in (2 * j, 2 * j + 1):
                    if scatter_path(t)[0] == "x":
                        scatter_send(t, 0, hh)
                    elif hh == (0 if Y == 2 else 1):
                        scatter_send(t, 0)

            def scatter_event(k, j):
                ts = (2 * j, 2 * j + 1) + (("bias",) if j == 0 else ())
                for t in ts:
                    scatter_wait(t, k - 1)
                    scatter_add(t, k - 1)
                    if k < 3:
                        scatter_send(t, k)

            def store_part(s):
                j, hh = s // 2, s % 2
                ys = pl.ds(half_of(hh) * half_y, half_y)
                return pltpu.make_async_copy(
                    pt.at[j, ys],
                    gw_hbm.at[ys, :, :, :, pl.ds(pl.multiple_of(j * PC, PC), PC)],
                    lsem.at[12 + panels + s],
                )

            for d in range(n_dev if linked else 0):
                col = pl.ds(d * R // 128 * 128, 128)
                ptb[d // (X * 2 * S), d // (2 * S) % X, d // S % 2, d % S] = gbacc[:, col]
            if linked:
                send(
                    ("swap", "bias"),
                    lambda: (ptb.at[:, :, 1 - c], crb, me.peer("c", 1)),
                )

            @pl.loop(0, 2 * panels)
            def _(s):
                j, hh = s // 2, s % 2
                h = half_of(hh)
                rows_ = pl.ds(pl.multiple_of(h * half_rows, half_rows), half_rows)
                col = pl.ds(pl.multiple_of(j * PC, PC), PC)
                total = dot(mixed[:, rows_], fg[:, col], TN).astype(BF16)
                pt[j, pl.ds(h * half_y, half_y)] = total.reshape(half_y, X, 2, SR, PC)
                if not linked:
                    store_part(s).start()
                    return
                swap(s).start()

                @pl.when(s == 0)
                def _():
                    arrived(("swap", "bias"), crb)
                    mine = ptb.at[:, :, c]
                    mine[...] = mine[...] + crb[...]
                    scatter_send("bias", 0)

                for e in range(2 * panels - 1):
                    pl.when(s == e + 1)(lambda e=e: core_sum(e))
                for at, k, panel in SUM_EVENTS:
                    pl.when(s == at)(lambda k=k, p=panel: scatter_event(k, p))

            def store_sp(s):
                i, yy = s // Y, s % Y
                slot = s % 2
                return pltpu.make_async_copy(
                    sp.at[slot],
                    sp_hbm.at[
                        pl.ds(pl.multiple_of(i * TM, TM), TM),
                        pl.ds(pl.multiple_of(yy * FW, FW), FW),
                    ],
                    lsem.at[slot],
                )

            steps = nodes // TM * Y

            @pl.loop(0, steps)
            def _(s):
                i, yy = s // Y, s % Y
                r = pl.ds(pl.multiple_of(i * TM, TM), TM)
                total = None
                for j in range(panels):
                    rhs = wg[j, yy].reshape(FW, PC)
                    term = dot(fg[r, pl.ds(j * PC, PC)], rhs, NT)
                    total = term if total is None else total + term
                scale = jnp.concatenate([fac[r, :]] * (FW // 128), axis=1)

                @pl.when(s >= 2)
                def _():
                    store_sp(s - 2).wait()

                sp[lax.rem(s, 2)] = (scale * total).astype(BF16)
                store_sp(s).start()
                if not linked:
                    return
                pl.when(s == 0)(lambda: core_sum(2 * panels - 1))
                for at, k, panel in BACK_EVENTS:
                    pl.when(s == at)(lambda k=k, p=panel: scatter_event(k, p))

            for s in (steps - 2, steps - 1):
                store_sp(s).wait()
            if linked:
                scatter_event(3, panels - 1)
                out_w = pltpu.make_async_copy(gws, gw_hbm, lsem.at[2])
                out_b = pltpu.make_async_copy(gbs, gb_hbm, lsem.at[3])
            else:
                for s in range(2 * panels):
                    store_part(s).wait()
                out_b = pltpu.make_async_copy(gbacc, gb_hbm, lsem.at[3])
            out_b.start()
            if linked:
                out_w.start()
                for s in range(2 * panels):
                    swap(s).wait_send()
                for name, make in started:
                    remote(name, *make()).wait_send()
                out_w.wait()
            out_b.wait()

        pl.run_scoped(
            back_phase,
            pltpu.VMEM((panels, Y, X, 2, SR, PC), BF16),
            pltpu.VMEM((2, TM, FW), BF16),
        )

    any_spec = pl.BlockSpec(memory_space=pl.ANY)
    scratch = [
        pltpu.VMEM((nodes, width), BF16),
        pltpu.VMEM((nodes, width), BF16),
        pltpu.VMEM((panels, Y, X, 2, SR, PC), BF16),
        pltpu.VMEM((clusters, CLUSTER, CLUSTER), BF16),
        pltpu.VMEM((nodes, 128), F32),
        pltpu.VMEM((Y, X, 2, S, 8, 128), F32),
        pltpu.VMEM((8, width), F32),
        pltpu.VMEM((8, width), F32),
        pltpu.VMEM((panels, Y, X, SR, PC), BF16),
        pltpu.VMEM((Y, X, S, 8, 128), F32),
        pltpu.VMEM((Y, X, 2, S, 8, 128), F32),
        pltpu.VMEM((R, width), F32),
        pltpu.VMEM((8, 128), F32),
        *stage_shapes(),
        pltpu.SemaphoreType.DMA((n_sems,)),
        pltpu.SemaphoreType.DMA((n_sems,)),
        pltpu.SemaphoreType.DMA((12 + 3 * panels,)),
    ]
    if not linked:
        for k in (5, 8, 9, 10, 11, 12, *range(13, 13 + n_stage)):
            scratch[k] = pltpu.VMEM((8, 128), F32)
        scratch[-3] = scratch[-2] = pltpu.SemaphoreType.DMA((1,))
    return pl.pallas_call(
        kernel,
        out_shape=(
            jax.ShapeDtypeStruct((nodes, width), BF16),
            jax.ShapeDtypeStruct((nodes, width), BF16),
            jax.ShapeDtypeStruct((clusters, CLUSTER, CLUSTER), BF16),
            jax.ShapeDtypeStruct((R, width), F32)
            if linked
            else jax.ShapeDtypeStruct((Y, X, 2, SR, width), BF16),
            jax.ShapeDtypeStruct((8, 128 if linked else width), F32),
        ),
        in_specs=[any_spec] * 5,
        out_specs=(any_spec,) * 5,
        scratch_shapes=scratch,
        compiler_params=pltpu.CompilerParams(
            collective_id=0 if linked else None,
            has_side_effects=True,
            vmem_limit_bytes=60 * 2**20,
        ),
        name="layer",
    )


def last_kernel(a_ref, sp_ref, act_in, out_ref, act_out, held, in_sem, out_sem):
    step = pl.program_id(0) * pl.num_programs(1) + pl.program_id(1)
    count, rows = held.shape[0], held.shape[1]

    def inward(k):
        part = act_in.at[pl.ds(k * rows, rows)]
        return pltpu.make_async_copy(part, held.at[k], in_sem.at[k])

    def outward(k):
        part = act_out.at[pl.ds(k * rows, rows)]
        return pltpu.make_async_copy(held.at[k], part, out_sem.at[k])

    @pl.when(step == 0)
    def _():
        for k in range(count):
            inward(k).start()

    out_ref[...] = dot(a_ref[0], sp_ref[...], NN)
    for k in range(count):

        @pl.when(step == k)
        def _():
            inward(k).wait()
            outward(k).start()

    @pl.when(step == count - 1)
    def _():
        for k in range(count):
            outward(k).wait()


def last(links, spread, act):
    nodes, width = spread.shape
    tile = 512
    steps = nodes // CLUSTER * (width // tile)
    return pl.pallas_call(
        last_kernel,
        out_shape=(
            jax.ShapeDtypeStruct((nodes, width), F32),
            jax.ShapeDtypeStruct((nodes, width), BF16),
        ),
        grid=(nodes // CLUSTER, width // tile),
        in_specs=[
            pl.BlockSpec((1, CLUSTER, CLUSTER), lambda i, j: (i, 0, 0)),
            pl.BlockSpec((CLUSTER, tile), lambda i, j: (i, j)),
            pl.BlockSpec(memory_space=pl.ANY),
        ],
        out_specs=(
            pl.BlockSpec((CLUSTER, tile), lambda i, j: (i, j)),
            pl.BlockSpec(memory_space=pl.ANY),
        ),
        scratch_shapes=[
            pltpu.VMEM((steps, nodes // steps, width), BF16),
            pltpu.SemaphoreType.DMA((steps,)),
            pltpu.SemaphoreType.DMA((steps,)),
        ],
        compiler_params=pltpu.CompilerParams(vmem_limit_bytes=60 * 2**20),
        name="features",
    )(links, spread, act)


def solution(mesh):
    dp_size, shard_size = mesh.shape["dp"], mesh.shape["shard"]

    def on_device(features, neighbors, weight, bias_terms, grad_out):
        nodes, width = features.shape
        rows = weight.shape[0]
        layer = make_kernel(dp_size, shard_size, rows, width, nodes)
        if not linkable(rows):
            both = ("dp", "shard")
            full = lax.all_gather(weight, both, axis=0, tiled=True)
            bias = lax.all_gather(bias_terms, both, axis=0, tiled=True).astype(F32)
            act, spread, links, parts, bias_sums = layer(
                features,
                neighbors,
                full.reshape(dp_size // 4, 2, 2, shard_size * rows, width),
                jnp.broadcast_to(bias, (8, width)),
                grad_out,
            )
            grad_features, output = last(links, spread, act)
            parts = parts.reshape(width, width).astype(F32)
            bias_sums = jnp.sum(bias_sums, axis=0)
            return (
                output,
                grad_features,
                lax.psum_scatter(parts, both, scatter_dimension=0, tiled=True),
                lax.psum_scatter(bias_sums, both, scatter_dimension=0, tiled=True),
            )
        device = lax.axis_index("dp") * shard_size + lax.axis_index("shard")
        lane = lax.rem(device * rows, 128)
        bias_tile = lax.dynamic_update_slice(
            jnp.zeros((8, 128), F32),
            jnp.broadcast_to(bias_terms.astype(F32), (8, rows)),
            (0, lane),
        )
        act, spread, links, grad_weight, bias_sums = layer(
            features, neighbors, weight, bias_tile, grad_out
        )
        grad_features, output = last(links, spread, act)
        grad_bias = lax.dynamic_slice(jnp.sum(bias_sums, axis=0), (lane,), (rows,))
        return output, grad_features, grad_weight, grad_bias

    split = P(("dp", "shard"), None)
    flat = P(("dp", "shard"))
    return jax.shard_map(
        on_device,
        mesh=mesh,
        in_specs=(split, split, split, flat, split),
        out_specs=(split, split, split, flat),
        check_vma=False,
    )
```

```python
import jax
import jax.numpy as jnp
from jax import lax
from jax.experimental import pallas as pl
from jax.experimental.pallas import tpu as pltpu
from jax.sharding import PartitionSpec as P

F32, BF16, I32 = jnp.float32, jnp.bfloat16, jnp.int32
MESH = pl.DeviceIdType.MESH
CLUSTER = 1024
SLOTS = 128
UNROLL = 32
LOW = 64
PC = 512
HC = 256
ALPHA = 0.7978845608028654
BETA = ALPHA * 0.044715
NN = (((1,), (0,)), ((), ()))
TN = (((0,), (0,)), ((), ()))
NT = (((1,), (1,)), ((), ()))
ALL = slice(None)

GATHER = ("zxy", "zyx", "zxy", "zyx", "zxy", "zyx", "xzy", "yzx")
SCATTER = ("yzx", "xzy", "yxz", "xyz", "yxz", "xyz", "yxz", "xyz")
COUNT_EVENTS = (
    (4, "second", 0),
    (6, "first", 2),
    (8, "third", 0),
    (8, "second", 1),
    (12, "second", 3),
    (12, "second", 2),
)
MIX_EVENTS = (
    (0, "third", 1),
    (0, "pass", 0),
    (3, "third", 2),
    (7, "third", 3),
    (7, "pass", 1),
)
PANEL_GATHER = ((2, "ready", 1), (4, "pass", 2), (6, "ready", 2), (6, "pass", 3), (10, "ready", 3))
PANEL_CORE = ((7, 0), (9, 1), (11, 2), (13, 3), (15, 4), (17, 5))
PANEL_SCATTER = ((11, 1, 0), (15, 1, 1), (17, 2, 0), (17, 2, 1))
BACK_CORE = ((0, 6), (1, 7))
BACK_SCATTER = (
    (1, 3, 0),
    (2, 1, 2),
    (2, 3, 1),
    (4, 2, 2),
    (4, 1, 3),
    (6, 3, 2),
    (6, 2, 3),
)


def dot(a, b, dims):
    return lax.dot_general(a, b, dims, preferred_element_type=F32)


class Place:
    def __init__(self, dp_size, shard_size):
        dp, self.z = lax.axis_index("dp"), lax.axis_index("shard")
        self.dp = dp
        self.c, self.x, self.y = dp % 2, (dp // 2) % 2, dp // 4
        self.size = {"c": 2, "x": 2, "y": dp_size // 4, "z": shard_size}

    def at(self, dim):
        return {"c": self.c, "x": self.x, "y": self.y, "z": self.z}[dim]

    def shifted(self, dim, offset):
        size = self.size[dim]
        return lax.rem(self.at(dim) + (offset + size), size)

    def peer(self, dim, offset):
        other = self.shifted(dim, offset)
        if dim == "z":
            return (self.dp, other)
        step = {"c": 1, "x": 2, "y": 4}[dim]
        return (self.dp + step * (other - self.at(dim)), self.z)

    def lane(self, rows):
        return (self.dp * self.size["z"] + self.z) * rows % 128

    def offsets(self, dim):
        return range(1, self.size[dim])


class Sems:
    def __init__(self):
        self.index = {}

    def __getitem__(self, name):
        return self.index.setdefault(name, len(self.index))


def sem_names(sizes):
    sems = Sems()
    for t in list(range(len(GATHER))) + ["bias"]:
        path = GATHER[0] if t == "bias" else GATHER[t]
        for k in range(3):
            for o in range(1, sizes[path[k]]):
                sems["gather", t, k, o]
        sems["core", t, 0]
        for o in range(1, sizes[path[2]]):
            sems["core", t, o]
    for t in list(range(len(SCATTER))) + ["bias"]:
        path = SCATTER[0] if t == "bias" else SCATTER[t]
        for k in range(3):
            for o in range(1, sizes[path[k]]):
                for h in range(2 if k == 0 and path[0] == "x" else 1):
                    sems["scatter", t, k, o, h]
    sems["swap", "bias"]
    for s in range(len(SCATTER)):
        sems["swap", s]
    return sems


def linkable(rows):
    return rows % 16 == 0


def make_kernel(dp_size, shard_size, rows, width, nodes):
    sizes = {"c": 2, "x": 2, "y": dp_size // 4, "z": shard_size}
    Y, X, S, R = sizes["y"], 2, shard_size, rows
    SR = S * R
    n_dev = dp_size * shard_size
    panels = width // PC
    half_rows = width // 2
    clusters = nodes // CLUSTER
    sems = sem_names(sizes)
    n_sems = len(sems.index)
    chunks = nodes // 128
    TM = 512
    tiles = (nodes // TM) * panels
    per_panel = nodes // TM
    BM = 256

    def stage_shape(path, k):
        n = sizes[path[k]] - 1
        left = path[k + 1 :]
        lead = tuple(sizes[d] for d in "yx" if d in left)
        return (n,) + lead, ("z" in left)

    def stage_shapes():
        out = []
        for t in range(len(SCATTER)):
            for k in range(3):
                lead, z = stage_shape(SCATTER[t], k)
                out.append(pltpu.VMEM(lead + (SR if z else R, HC), BF16))
        for k in range(3):
            lead, z = stage_shape(SCATTER[0], k)
            out.append(pltpu.VMEM(lead + (S if z else 1, 8, 128), F32))
        return out

    n_stage = 3 * (len(SCATTER) + 1)
    linked = linkable(rows)

    def kernel(
        f_hbm, n_hbm, w_hbm, b_in, g_hbm,
        act_hbm, fg, a2t, gw_out, gb_out,
        mixed, wg, fac, b_own, bt, brow, gbacc, cr, crb, ptb, *rest,
    ):
        stage = rest[:n_stage]
        ssem, rsem, lsem = rest[n_stage:]
        me = Place(dp_size, shard_size)
        c, x, y, z = me.c, me.x, me.y, me.z
        started = {}

        def remote(name, src, dst, device):
            i = sems[name]
            return pltpu.make_async_remote_copy(
                src_ref=src, dst_ref=dst, send_sem=ssem.at[i], recv_sem=rsem.at[i],
                device_id=device, device_id_type=MESH,
            )

        def send(name, make):
            remote(name, *make()).start()
            started[name] = make

        def arrived(name, ref):
            remote(name, ref, ref, me.peer("c", 1)).wait_recv()

        def view(t, core, **at):
            ys, xs = at.get("y", ALL), at.get("x", ALL)
            if t == "bias":
                zs = pl.ds(at["z"], 1) if "z" in at else ALL
                return bt.at[ys, xs, core, zs]
            zs = pl.ds(pl.multiple_of(at["z"] * R, R), R) if "z" in at else ALL
            return wg.at[t // 2, ys, xs, core, zs, pl.ds(t % 2 * HC, HC)]

        own = {"x": x, "y": y, "z": z}

        def fixed(dims):
            return {d: own[d] for d in dims}

        def gather_path(t):
            return GATHER[0] if t == "bias" else GATHER[t]

        def gather_first(t):
            path = gather_path(t)

            def make(o):
                if t == "bias":
                    return b_own, bt.at[y, x, c, z], me.peer(path[0], o)
                src = w_hbm.at[:, pl.ds(t * HC, HC)]
                return src, view(t, c, **fixed("xyz")), me.peer(path[0], o)

            for o in me.offsets(path[0]):
                send(("gather", t, 0, o), lambda o=o: make(o))

        def gather_wait(t, k):
            path = gather_path(t)
            for o in me.offsets(path[k]):
                at = fixed(path[k:])
                at[path[k]] = me.shifted(path[k], -o)
                arrived(("gather", t, k, o), view(t, c, **at))

        def gather_send(t, k):
            path = gather_path(t)

            def make(o):
                ref = view(t, c, **fixed(path[k:]))
                return ref, ref, me.peer(path[k], o)

            for o in me.offsets(path[k]):
                send(("gather", t, k, o), lambda o=o: make(o))

        def core_send(t, late):
            path = gather_path(t)

            def make(o):
                at = {path[2]: me.shifted(path[2], -o)} if o else fixed(path[2:])
                ref = view(t, c, **at)
                return ref, ref, me.peer("c", 1)

            for o in me.offsets(path[2]) if late else (0,):
                send(("core", t, o), lambda o=o: make(o))

        def core_wait(t):
            path = gather_path(t)
            arrived(("core", t, 0), view(t, 1 - c, **fixed(path[2:])))
            for o in me.offsets(path[2]):
                arrived(
                    ("core", t, o),
                    view(t, 1 - c, **{path[2]: me.shifted(path[2], -o)}),
                )

        def slices(panel):
            return (2 * panel, 2 * panel + 1) + (("bias",) if panel == 0 else ())

        def own_block(j):
            if not linked:
                return pltpu.make_async_copy(
                    w_hbm.at[:, :, :, :, pl.ds(j * PC, PC)], wg.at[j], lsem.at[8 + j]
                )
            return pltpu.make_async_copy(
                w_hbm.at[:, pl.ds(j * PC, PC)],
                wg.at[j, y, x, c, pl.ds(pl.multiple_of(z * R, R), R), :],
                lsem.at[8 + j],
            )

        def own_bias():
            return pltpu.make_async_copy(b_own, bt.at[y, x, c, z], lsem.at[8 + panels])

        def gather_event(kind, panel):
            if not linked:
                if kind == "ready":
                    own_block(panel).wait()
            elif kind == "first":
                for t in slices(panel):
                    gather_first(t)
            elif kind == "second":
                for t in slices(panel):
                    gather_wait(t, 0)
                own_block(panel).wait()
                if panel == 0:
                    own_bias().wait()
                for t in slices(panel):
                    gather_send(t, 1)
            elif kind == "third":
                for t in slices(panel):
                    gather_wait(t, 1)
                for t in slices(panel):
                    gather_send(t, 2)
                for t in slices(panel):
                    core_send(t, False)
            elif kind == "pass":
                for t in slices(panel):
                    gather_wait(t, 2)
                for t in slices(panel):
                    core_send(t, True)
            elif kind == "ready":
                for t in slices(panel):
                    core_wait(t)

        load_n = lambda ref: pltpu.make_async_copy(n_hbm, ref, lsem.at[9 + panels])
        load_f = pltpu.make_async_copy(f_hbm, fg, lsem.at[10 + panels])

        def count_phase(nb, low, *digits):
            load_n(nb).start()
            peers = [me.peer(d, o) for d in "cxyz" for o in me.offsets(d) if linked]
            for p in peers:
                pl.semaphore_signal(
                    pltpu.get_barrier_semaphore(), inc=1,
                    device_id=p, device_id_type=MESH,
                )
            for j in range(panels):
                own_block(j).start()
            if linked:
                bias = b_in[...].astype(F32)
                bias = jnp.concatenate([bias, jnp.zeros((1, 128 - R), F32)], axis=1)
                bias = jnp.broadcast_to(bias, (8, 128))
                b_own[...] = pltpu.roll(bias, me.lane(R), 1)
                own_bias().start()
                pl.semaphore_wait(pltpu.get_barrier_semaphore(), len(peers))
            gather_event("first", 0)
            gather_event("first", 3)
            load_f.start()
            load_n(nb).wait()

            @pl.loop(0, chunks)
            def _(q):
                r = pl.ds(pl.multiple_of(q * 128, 128), 128)
                ids = nb[r, :]
                degree = jnp.sum((ids >= 0).astype(F32), axis=1, keepdims=True)
                fac[r, :] = jnp.broadcast_to(1.0 / (degree + 1.0), (128, 128))
                ids = ids.T
                high = ids >> (LOW.bit_length() - 1)
                digit = jnp.left_shift(jnp.ones_like(ids), (high & 3) * 8)
                low[:, r] = ids & (LOW - 1)
                for k, ref in enumerate(digits):
                    ref[:, r] = jnp.where(high >> 2 == k, digit, 0)

            gather_event("first", 1)
            place_in = lax.broadcasted_iota(I32, (LOW, 128), 0)
            lane = lax.broadcasted_iota(I32, (LOW, 128), 1)

            @pl.loop(0, chunks)
            def _(q):
                col = pl.ds(pl.multiple_of(q * 128, 128), 128)

                def step(s, carry):
                    some = pl.ds(pl.multiple_of(s * UNROLL, UNROLL), UNROLL)
                    lo, add = low[some, col], [ref[some, col] for ref in digits]
                    for k in range(UNROLL):
                        hit = lo[k : k + 1] == place_in
                        carry = tuple(
                            total + jnp.where(hit, a[k : k + 1], 0)
                            for total, a in zip(carry, add)
                        )
                    return carry

                zero = (jnp.zeros((LOW, 128), I32),) * len(digits)
                totals = lax.fori_loop(0, SLOTS // UNROLL, step, zero)
                cl, place = q // 8, q % 8
                to = pl.ds(pl.multiple_of(place * 128, 128), 128)
                for b in range(CLUSTER // LOW):
                    count = ((totals[b // 4] >> (8 * (b % 4))) & 255).astype(F32)
                    self_at = place * 128 - b * LOW
                    count = count + jnp.where(place_in - lane == self_at, 2.0, 0.0)
                    a2t[cl, pl.ds(b * LOW, LOW), to] = count.astype(BF16)
                for at, kind, panel in COUNT_EVENTS:
                    pl.when(q == at)(lambda k=kind, p=panel: gather_event(k, p))

        pl.run_scoped(
            count_phase,
            pltpu.VMEM((nodes, SLOTS), I32),
            *[pltpu.VMEM((SLOTS, nodes), I32)] * (1 + CLUSTER // LOW // 4),
        )
        load_f.wait()

        @pl.loop(0, clusters * 4)
        def _(s):
            cl, i, j = s // 4, (s // 2) % 2, s % 2
            r = pl.ds(pl.multiple_of(cl * CLUSTER + i * 512, 512), 512)
            k = pl.ds(pl.multiple_of(cl * CLUSTER, CLUSTER), CLUSTER)
            col = pl.ds(pl.multiple_of(j * half_rows, half_rows), half_rows)
            links = a2t[cl, :, pl.ds(pl.multiple_of(i * 512, 512), 512)]
            total = dot(links, fg[k, col], TN)
            scale = jnp.concatenate([fac[r, :]] * (half_rows // 128), axis=1)
            mixed[r, col] = (scale * total).astype(BF16)
            for at, kind, panel in MIX_EVENTS:
                pl.when(s == at)(lambda k=kind, p=panel: gather_event(k, p))

        half_y = Y // 2
        y_half = y // half_y

        def half_of(hh):
            if isinstance(hh, int):
                return y_half if hh else 1 - y_half
            return jnp.where(hh == 0, 1 - y_half, y_half)

        def part(pt, t, core, **at):
            ys, xs = at.get("y", ALL), at.get("x", ALL)
            if t == "bias":
                zs = pl.ds(at["z"], 1) if "z" in at else ALL
                return ptb.at[ys, xs, core, zs]
            zs = pl.ds(pl.multiple_of(at["z"] * R, R), R) if "z" in at else ALL
            return pt.at[t // 2, ys, xs, core, zs, pl.ds(t % 2 * HC, HC)]

        def scatter_path(t):
            return SCATTER[0] if t == "bias" else SCATTER[t]

        def landing(t, k):
            return stage[(len(SCATTER) if t == "bias" else t) * 3 + k]

        def scatter_send(pt, t, k, h=None):
            path = scatter_path(t)

            def make(o):
                at = fixed(path[:k])
                at[path[k]] = me.shifted(path[k], o)
                dst = landing(t, k).at[o - 1]
                if h is not None:
                    ys = pl.ds(half_of(h) * half_y, half_y)
                    at["y"] = ys
                    dst = dst.at[ys]
                return part(pt, t, c, **at), dst, me.peer(path[k], o)

            for o in me.offsets(path[k]):
                send(("scatter", t, k, o, h or 0), lambda o=o: make(o))

        def scatter_wait(t, k):
            path = scatter_path(t)
            for o in me.offsets(path[k]):
                ref = landing(t, k).at[o - 1]
                if t != "bias" and k == 0 and path[0] == "x":
                    for i in range(2):
                        ys = pl.ds(half_of(i) * half_y, half_y)
                        arrived(("scatter", t, k, o, i), ref.at[ys])
                else:
                    arrived(("scatter", t, k, o, 0), ref)

        def scatter_add(pt, t, k):
            path = scatter_path(t)
            mine = part(pt, t, c, **fixed(path[: k + 1]))
            total = mine[...].astype(F32)
            for o in me.offsets(path[k]):
                total = total + landing(t, k)[o - 1].astype(F32)
            if k < 2:
                mine[...] = total.astype(mine.dtype)
            elif t == "bias":
                gb_out[...] = total.reshape(8, 128)
            else:
                gw_out[:, pl.ds(t * HC, HC)] = total

        def swap(pt, s):
            j, hh = s // 2, s % 2
            ys = pl.ds(half_of(hh) * half_y, half_y)
            i = sems["swap", 0] + s
            return pltpu.make_async_remote_copy(
                src_ref=pt.at[j, ys, :, 1 - c], dst_ref=cr.at[j, ys],
                send_sem=ssem.at[i], recv_sem=rsem.at[i],
                device_id=me.peer("c", 1), device_id_type=MESH,
            )

        def core_sum(pt, s):
            j, hh = s // 2, s % 2
            swap(pt, s).wait_recv()
            ys = pl.ds(half_of(hh) * half_y, half_y)
            mine = pt.at[j, ys, :, c]
            mine[...] = (mine[...].astype(F32) + cr[j, ys].astype(F32)).astype(BF16)
            for t in (2 * j, 2 * j + 1):
                if scatter_path(t)[0] == "x":
                    scatter_send(pt, t, 0, hh)
                elif hh == (0 if Y == 2 else 1):
                    scatter_send(pt, t, 0)

        def scatter_event(pt, k, j):
            ts = (2 * j, 2 * j + 1) + (("bias",) if j == panels - 2 else ())
            for t in ts:
                scatter_wait(t, k - 1)
                scatter_add(pt, t, k - 1)
                if k < 3:
                    scatter_send(pt, t, k)

        def store_part(pt, s):
            j, hh = s // 2, s % 2
            ys = pl.ds(half_of(hh) * half_y, half_y)
            return pltpu.make_async_copy(
                pt.at[j, ys],
                gw_out.at[ys, :, :, :, pl.ds(pl.multiple_of(j * PC, PC), PC)],
                lsem.at[12 + panels + s],
            )

        def panel_phase(pt, acc_a, acc_b, go, ac):
            def block(hbm, j, i):
                return hbm.at[
                    pl.ds(i * TM, TM), pl.ds(pl.multiple_of(j * PC, PC), PC)
                ]

            def load_g(j, i):
                return pltpu.make_async_copy(block(g_hbm, j, i), go.at[i], lsem.at[i])

            def store_act(j, i):
                return pltpu.make_async_copy(
                    ac.at[i], block(act_hbm, j, i), lsem.at[4 + i]
                )

            def product(j, i):
                panel = wg[j].reshape(width, PC)
                return dot(mixed[pl.ds(i * TM, TM), :], panel, NN)

            def finish(acc, j, i):
                r = pl.ds(i * TM, TM)
                col = pl.ds(pl.multiple_of(j * PC, PC), PC)
                v = acc[...] + brow[0:1, col]
                u = v * v
                h = 0.5 + 0.5 * jnp.tanh(v * (ALPHA + BETA * u))
                a = v * h
                d = h + (a * (1.0 - h)) * (2 * ALPHA + (6 * BETA) * u)
                g = go[i].astype(F32) * d
                ac[i] = a.astype(BF16)
                fg[r, col] = g.astype(BF16)
                gbacc[:, col] += jnp.sum(g.reshape(TM // 8, 8, PC), axis=0)

            def weight_tile(j, hh):
                h = half_of(hh)
                rows_ = pl.ds(pl.multiple_of(h * half_rows, half_rows), half_rows)
                col = pl.ds(pl.multiple_of(j * PC, PC), PC)
                total = dot(mixed[:, rows_], fg[:, col], TN).astype(BF16)
                pt[j, pl.ds(h * half_y, half_y)] = total.reshape(half_y, X, 2, SR, PC)

            def leave(j, hh):
                if linked:
                    swap(pt, 2 * j + hh).start()
                else:
                    store_part(pt, 2 * j + hh).start()

            def before(j, i, first):
                load_g(j, i).wait()
                if not first:
                    store_act(j - 1, i).wait()

            def after(j, i, last):
                store_act(j, i).start()
                if not last:
                    load_g(j + 1, i).start()

            def events(step, fixed_step=None):
                def run(at, action):
                    if fixed_step is None:
                        if 4 <= at < 4 * (panels - 1):
                            pl.when(step == at)(action)
                    elif fixed_step == at:
                        action()

                for at, kind, panel in PANEL_GATHER:
                    run(at, lambda k=kind, p=panel: gather_event(k, p))
                if not linked:
                    return
                for at, e in PANEL_CORE:
                    run(at, lambda e=e: core_sum(pt, e))
                for at, k, panel in PANEL_SCATTER:
                    run(at, lambda k=k, p=panel: scatter_event(pt, k, p))

            def panel(j, first, last):
                steps = [4 * j + b for b in range(4)]

                def done(b):
                    if first or last:
                        events(None, steps[b])
                    else:
                        events(steps[b])

                before(j, 0, first)
                acc_b[...] = product(j, 1)
                finish(acc_a, j, 0)
                after(j, 0, last)
                done(0)
                before(j, 1, first)
                if not first:
                    weight_tile(j - 1, 0)
                finish(acc_b, j, 1)
                acc_a[...] = product(j, 2)
                after(j, 1, last)
                if not first:
                    leave(j - 1, 0)
                done(1)
                before(j, 2, first)
                acc_b[...] = product(j, 3)
                finish(acc_a, j, 2)
                after(j, 2, last)
                done(2)
                before(j, 3, first)
                if not first:
                    weight_tile(j - 1, 1)
                finish(acc_b, j, 3)
                if not last:
                    acc_a[...] = product(j + 1, 0)
                after(j, 3, last)
                if not first:
                    leave(j - 1, 1)
                done(3)

            for i in range(per_panel):
                load_g(0, i).start()
            gather_event("ready", 0)
            p = 128 // R
            if not linked:
                brow[...] = b_in[...]
            for k in range(width // 128 if linked else 0):
                tile = jnp.zeros((8, 128), F32)
                for d in range(k * p, (k + 1) * p):
                    tile = tile + bt[d // (X * 2 * S), d // (2 * S) % X, d // S % 2, d % S]
                brow[:, pl.ds(k * 128, 128)] = tile
            gbacc[...] = jnp.zeros_like(gbacc)
            acc_a[...] = product(0, 0)
            panel(0, True, False)
            pl.loop(1, panels - 1)(lambda j: panel(j, False, False))
            panel(panels - 1, False, True)
            if linked:
                for d in range(n_dev):
                    col = pl.ds(d * R // 128 * 128, 128)
                    at = (d // (X * 2 * S), d // (2 * S) % X, d // S % 2, d % S)
                    ptb[at] = gbacc[:, col]
                send(
                    ("swap", "bias"),
                    lambda: (ptb.at[:, :, 1 - c], crb, me.peer("c", 1)),
                )
            weight_tile(panels - 1, 0)
            leave(panels - 1, 0)
            events(None, 4 * panels)
            weight_tile(panels - 1, 1)
            leave(panels - 1, 1)
            if linked:
                arrived(("swap", "bias"), crb)
                mine = ptb.at[:, :, c]
                mine[...] = mine[...] + crb[...]
                scatter_send(pt, "bias", 0)
            events(None, 4 * panels + 1)
            for i in range(per_panel):
                store_act(panels - 1, i).wait()

        def back_phase(pt):
            steps = nodes // BM

            @pl.loop(0, steps)
            def _(s):
                r = pl.ds(pl.multiple_of(s * BM, BM), BM)
                total = None
                for j in range(panels):
                    rhs = wg[j].reshape(width, PC)
                    term = dot(fg[r, pl.ds(j * PC, PC)], rhs, NT)
                    total = term if total is None else total + term
                scale = jnp.concatenate([fac[r, :]] * (width // 128), axis=1)
                fg[r, :] = (scale * total).astype(BF16)
                if not linked:
                    return
                for at, e in BACK_CORE:
                    pl.when(s == at)(lambda e=e: core_sum(pt, e))
                for at, k, panel in BACK_SCATTER:
                    pl.when(s == at)(lambda k=k, p=panel: scatter_event(pt, k, p))

            if linked:
                scatter_event(pt, 3, panels - 1)
                for s in range(2 * panels):
                    swap(pt, s).wait_send()
                for name, make in started.items():
                    remote(name, *make()).wait_send()
            else:
                for s in range(2 * panels):
                    store_part(pt, s).wait()
                gb_out[...] = gbacc[...]

        def with_parts(pt):
            pl.run_scoped(
                lambda *refs: panel_phase(pt, *refs),
                *[pltpu.VMEM((TM, PC), F32)] * 2,
                *[pltpu.VMEM((per_panel, TM, PC), BF16)] * 2,
            )
            back_phase(pt)

        pl.run_scoped(with_parts, pltpu.VMEM((panels, Y, X, 2, SR, PC), BF16))

    away = pl.BlockSpec(memory_space=pltpu.HBM)
    here = pl.BlockSpec(memory_space=pltpu.VMEM)
    scratch = [
        pltpu.VMEM((nodes, width), BF16),
        pltpu.VMEM((panels, Y, X, 2, SR, PC), BF16),
        pltpu.VMEM((nodes, 128), F32),
        pltpu.VMEM((8, 128), F32),
        pltpu.VMEM((Y, X, 2, S, 8, 128), F32),
        pltpu.VMEM((8, width), F32),
        pltpu.VMEM((8, width), F32),
        pltpu.VMEM((panels, Y, X, SR, PC), BF16),
        pltpu.VMEM((Y, X, S, 8, 128), F32),
        pltpu.VMEM((Y, X, 2, S, 8, 128), F32),
        *stage_shapes(),
        pltpu.SemaphoreType.DMA((n_sems,)),
        pltpu.SemaphoreType.DMA((n_sems,)),
        pltpu.SemaphoreType.DMA((12 + 3 * panels,)),
    ]
    if not linked:
        for k in (3, 4, 7, 8, 9, *range(10, 10 + n_stage)):
            scratch[k] = pltpu.VMEM((8, 128), F32)
        scratch[-3] = scratch[-2] = pltpu.SemaphoreType.DMA((1,))
    return pl.pallas_call(
        kernel,
        out_shape=(
            jax.ShapeDtypeStruct((nodes, width), BF16),
            pltpu.VMEM((nodes, width), BF16),
            pltpu.VMEM((clusters, CLUSTER, CLUSTER), BF16),
            pltpu.VMEM((R, width), F32)
            if linked
            else jax.ShapeDtypeStruct((Y, X, 2, SR, width), BF16),
            pltpu.VMEM((8, 128 if linked else width), F32),
        ),
        in_specs=[away] * 3 + [here, away],
        out_specs=(away, here, here, here if linked else away, here),
        scratch_shapes=scratch,
        compiler_params=pltpu.CompilerParams(
            collective_id=0 if linked else None,
            has_side_effects=True,
            vmem_limit_bytes=48 * 2**20,
        ),
        name="layer",
    )


def make_last(dp_size, shard_size, rows, width, nodes):
    clusters = nodes // CLUSTER
    per_cluster = width // PC
    steps = clusters * per_cluster
    part_rows = nodes // steps
    linked = linkable(rows)

    def kernel(links, spread, act_in, gw_in, gb_in, out, act_out, gw_out, gb_out, held, tiles, sem):
        def inward(k):
            part = act_in.at[pl.ds(k * part_rows, part_rows)]
            return pltpu.make_async_copy(part, held.at[k], sem.at[k])

        def outward(k):
            part = act_out.at[pl.ds(k * part_rows, part_rows)]
            return pltpu.make_async_copy(held.at[k], part, sem.at[steps + k])

        def store(k):
            at = (
                pl.ds(k // per_cluster * CLUSTER, CLUSTER),
                pl.ds(k % per_cluster * PC, PC),
            )
            return pltpu.make_async_copy(
                tiles.at[k % 2], out.at[at], sem.at[2 * steps + k % 2]
            )

        carry = pltpu.make_async_copy(gw_in, gw_out, sem.at[2 * steps + 2])
        for k in range(steps):
            inward(k).start()
        if linked:
            carry.start()
            me = Place(dp_size, shard_size)
            total = jnp.sum(gb_in[...], axis=0, keepdims=True)
            total = jnp.broadcast_to(total, (8, 128))
            gb_out[...] = pltpu.roll(total, (128 - me.lane(rows)) % 128, 1)[0:1, :rows]
        for k in range(steps):
            cl = k // per_cluster
            some = spread[pl.ds(cl * CLUSTER, CLUSTER), pl.ds(k % per_cluster * PC, PC)]
            if k >= 2:
                store(k - 2).wait()
            tiles[k % 2] = dot(links[cl], some, NN)
            store(k).start()
            inward(k).wait()
            outward(k).start()
        for k in range(steps):
            outward(k).wait()
        for k in (steps - 2, steps - 1):
            store(k).wait()
        if linked:
            carry.wait()

    away = pl.BlockSpec(memory_space=pltpu.HBM)
    here = pl.BlockSpec(memory_space=pltpu.VMEM)
    return pl.pallas_call(
        kernel,
        out_shape=(
            jax.ShapeDtypeStruct((nodes, width), F32),
            jax.ShapeDtypeStruct((nodes, width), BF16),
            jax.ShapeDtypeStruct((rows, width), F32),
            jax.ShapeDtypeStruct((1, rows), F32),
        ),
        in_specs=[here, here, away, here, here],
        out_specs=(away, away, away, here),
        scratch_shapes=[
            pltpu.VMEM((steps, part_rows, width), BF16),
            pltpu.VMEM((2, CLUSTER, PC), F32),
            pltpu.SemaphoreType.DMA((2 * steps + 3,)),
        ],
        compiler_params=pltpu.CompilerParams(vmem_limit_bytes=14 * 2**20),
        name="features",
    )


def solution(mesh):
    dp_size, shard_size = mesh.shape["dp"], mesh.shape["shard"]

    def keep(array):
        return pltpu.with_memory_space_constraint(array, pltpu.VMEM)

    def leave(array):
        return pltpu.with_memory_space_constraint(array, pltpu.HBM)

    def on_device(features, neighbors, weight, bias_terms, grad_out):
        nodes, width = features.shape
        rows = weight.shape[0]
        layer = make_kernel(dp_size, shard_size, rows, width, nodes)
        last = make_last(dp_size, shard_size, rows, width, nodes)
        if linkable(rows):
            act, spread, links, grad_weight, bias_sums = layer(
                features, neighbors, weight, bias_terms.reshape(1, rows), grad_out
            )
            grad_features, output, grad_weight, grad_bias = last(
                keep(links), keep(spread), leave(act), keep(grad_weight), keep(bias_sums)
            )
            return output, grad_features, grad_weight, grad_bias.reshape(rows)
        both = ("dp", "shard")
        full = lax.all_gather(weight, both, axis=0, tiled=True)
        bias = lax.all_gather(bias_terms, both, axis=0, tiled=True).astype(F32)
        act, spread, links, parts, bias_sums = layer(
            features,
            neighbors,
            full.reshape(dp_size // 4, 2, 2, shard_size * rows, width),
            jnp.broadcast_to(bias, (8, width)),
            grad_out,
        )
        grad_features, output, *_ = last(
            keep(links),
            keep(spread),
            leave(act),
            jnp.zeros((rows, width), F32),
            jnp.zeros((8, 128), F32),
        )
        parts = parts.reshape(width, width).astype(F32)
        bias_sums = jnp.sum(bias_sums, axis=0)
        return (
            output,
            grad_features,
            lax.psum_scatter(parts, both, scatter_dimension=0, tiled=True),
            lax.psum_scatter(bias_sums, both, scatter_dimension=0, tiled=True),
        )

    split = P(("dp", "shard"), None)
    flat = P(("dp", "shard"))
    return jax.shard_map(
        on_device,
        mesh=mesh,
        in_specs=(split, split, split, flat, split),
        out_specs=(split, split, split, flat),
        check_vma=False,
    )
```

```python
import jax
import jax.numpy as jnp
from jax import lax
from jax.experimental import pallas as pl
from jax.experimental.pallas import tpu as pltpu
from jax.sharding import PartitionSpec as P

F32, BF16, I32 = jnp.float32, jnp.bfloat16, jnp.int32
MESH = pl.DeviceIdType.MESH
CLUSTER = 1024
SLOTS = 128
UNROLL = 32
LOW = 64
PC = 512
HC = 256
ALPHA = 0.7978845608028654
BETA = ALPHA * 0.044715
NN = (((1,), (0,)), ((), ()))
TN = (((0,), (0,)), ((), ()))
NT = (((1,), (1,)), ((), ()))
ALL = slice(None)

GATHER = ("zxy", "zyx", "zxy", "zyx", "zxy", "zyx", "xzy", "yzx")
SCATTER = ("yzx", "xzy", "yxz", "xyz", "yxz", "xyz", "yxz", "xyz")
COUNT_EVENTS = (
    (4, "second", 0),
    (6, "first", 2),
    (8, "third", 0),
    (8, "second", 1),
    (12, "second", 3),
    (12, "second", 2),
)
MIX_EVENTS = (
    (0, "third", 1),
    (0, "pass", 0),
    (3, "third", 2),
    (7, "third", 3),
    (7, "pass", 1),
)
PANEL_GATHER = (
    (0, "ready", 1),
    (1, "pass", 2),
    (4, "pass", 3),
    (4, "ready", 2),
    (8, "ready", 3),
)
PANEL_SCATTER = (
    (7, 1, 0),
    (11, 1, 1),
    (13, 2, 0),
    (14, 2, 1),
    (15, 1, 2),
)
BACK_SCATTER = (
    (0, 3, 0),
    (1, 3, 1),
    (1, 2, 2),
    (3, 1, 3),
    (3, 3, 2),
    (5, 2, 3),
)


def dot(a, b, dims):
    return lax.dot_general(a, b, dims, preferred_element_type=F32)


class Place:
    def __init__(self, dp_size, shard_size):
        dp, self.z = lax.axis_index("dp"), lax.axis_index("shard")
        self.dp = dp
        self.c, self.x, self.y = dp % 2, (dp // 2) % 2, dp // 4
        self.size = {"c": 2, "x": 2, "y": dp_size // 4, "z": shard_size}

    def at(self, dim):
        return {"c": self.c, "x": self.x, "y": self.y, "z": self.z}[dim]

    def shifted(self, dim, offset):
        size = self.size[dim]
        return lax.rem(self.at(dim) + (offset + size), size)

    def peer(self, dim, offset):
        other = self.shifted(dim, offset)
        if dim == "z":
            return (self.dp, other)
        step = {"c": 1, "x": 2, "y": 4}[dim]
        return (self.dp + step * (other - self.at(dim)), self.z)

    def lane(self, rows):
        return (self.dp * self.size["z"] + self.z) * rows % 128

    def offsets(self, dim):
        return range(1, self.size[dim])


class Sems:
    def __init__(self):
        self.index = {}

    def __getitem__(self, name):
        return self.index.setdefault(name, len(self.index))


def sem_names(sizes):
    sems = Sems()
    for t in list(range(len(GATHER))) + ["bias"]:
        path = GATHER[0] if t == "bias" else GATHER[t]
        for k in range(3):
            for o in range(1, sizes[path[k]]):
                sems["gather", t, k, o]
        sems["core", t, 0]
        for o in range(1, sizes[path[2]]):
            sems["core", t, o]
    for t in list(range(len(SCATTER))) + ["bias"]:
        path = SCATTER[0] if t == "bias" else SCATTER[t]
        for k in range(3):
            for o in range(1, sizes[path[k]]):
                for h in range(2 if k == 0 and path[0] == "x" else 1):
                    sems["scatter", t, k, o, h]
    sems["swap", "bias"]
    for s in range(len(SCATTER)):
        sems["swap", s]
    return sems


def linkable(rows):
    return rows % 16 == 0


def make_kernel(dp_size, shard_size, rows, width, nodes):
    sizes = {"c": 2, "x": 2, "y": dp_size // 4, "z": shard_size}
    Y, X, S, R = sizes["y"], 2, shard_size, rows
    SR = S * R
    n_dev = dp_size * shard_size
    panels = width // PC
    half_rows = width // 2
    clusters = nodes // CLUSTER
    sems = sem_names(sizes)
    n_sems = len(sems.index)
    chunks = nodes // 128
    TM = 512
    tiles = (nodes // TM) * panels
    per_panel = nodes // TM
    BM = 256

    def stage_shape(path, k):
        n = sizes[path[k]] - 1
        left = path[k + 1 :]
        lead = tuple(sizes[d] for d in "yx" if d in left)
        return (n,) + lead, ("z" in left)

    def stage_shapes():
        out = []
        for t in range(len(SCATTER)):
            for k in range(3):
                lead, z = stage_shape(SCATTER[t], k)
                out.append(pltpu.VMEM(lead + (SR if z else R, HC), BF16))
        for k in range(3):
            lead, z = stage_shape(SCATTER[0], k)
            out.append(pltpu.VMEM(lead + (S if z else 1, 8, 128), F32))
        return out

    n_stage = 3 * (len(SCATTER) + 1)
    linked = linkable(rows)

    def kernel(
        f_hbm, n_hbm, w_hbm, b_in, g_hbm,
        act_hbm, fg, a2t, gw_out, gb_out,
        mixed, wg, fac, b_own, bt, brow, gbacc, cr, crb, ptb, *rest,
    ):
        stage = rest[:n_stage]
        ssem, rsem, lsem = rest[n_stage:]
        me = Place(dp_size, shard_size)
        c, x, y, z = me.c, me.x, me.y, me.z
        started = {}

        def remote(name, src, dst, device):
            i = sems[name]
            return pltpu.make_async_remote_copy(
                src_ref=src, dst_ref=dst, send_sem=ssem.at[i], recv_sem=rsem.at[i],
                device_id=device, device_id_type=MESH,
            )

        def send(name, make):
            remote(name, *make()).start()
            started[name] = make

        def arrived(name, ref):
            remote(name, ref, ref, me.peer("c", 1)).wait_recv()

        def view(t, core, **at):
            ys, xs = at.get("y", ALL), at.get("x", ALL)
            if t == "bias":
                zs = pl.ds(at["z"], 1) if "z" in at else ALL
                return bt.at[ys, xs, core, zs]
            zs = pl.ds(pl.multiple_of(at["z"] * R, R), R) if "z" in at else ALL
            return wg.at[t // 2, ys, xs, core, zs, pl.ds(t % 2 * HC, HC)]

        own = {"x": x, "y": y, "z": z}

        def fixed(dims):
            return {d: own[d] for d in dims}

        def gather_path(t):
            return GATHER[0] if t == "bias" else GATHER[t]

        def gather_first(t):
            path = gather_path(t)

            def make(o):
                if t == "bias":
                    return b_own, bt.at[y, x, c, z], me.peer(path[0], o)
                src = w_hbm.at[:, pl.ds(t * HC, HC)]
                return src, view(t, c, **fixed("xyz")), me.peer(path[0], o)

            for o in me.offsets(path[0]):
                send(("gather", t, 0, o), lambda o=o: make(o))

        def gather_wait(t, k):
            path = gather_path(t)
            for o in me.offsets(path[k]):
                at = fixed(path[k:])
                at[path[k]] = me.shifted(path[k], -o)
                arrived(("gather", t, k, o), view(t, c, **at))

        def gather_send(t, k):
            path = gather_path(t)

            def make(o):
                ref = view(t, c, **fixed(path[k:]))
                return ref, ref, me.peer(path[k], o)

            for o in me.offsets(path[k]):
                send(("gather", t, k, o), lambda o=o: make(o))

        def core_send(t, late):
            path = gather_path(t)

            def make(o):
                at = {path[2]: me.shifted(path[2], -o)} if o else fixed(path[2:])
                ref = view(t, c, **at)
                return ref, ref, me.peer("c", 1)

            for o in me.offsets(path[2]) if late else (0,):
                send(("core", t, o), lambda o=o: make(o))

        def core_wait(t):
            path = gather_path(t)
            arrived(("core", t, 0), view(t, 1 - c, **fixed(path[2:])))
            for o in me.offsets(path[2]):
                arrived(
                    ("core", t, o),
                    view(t, 1 - c, **{path[2]: me.shifted(path[2], -o)}),
                )

        def slices(panel):
            return (2 * panel, 2 * panel + 1) + (("bias",) if panel == 0 else ())

        def own_block(j):
            if not linked:
                return pltpu.make_async_copy(
                    w_hbm.at[:, :, :, :, pl.ds(j * PC, PC)], wg.at[j], lsem.at[8 + j]
                )
            return pltpu.make_async_copy(
                w_hbm.at[:, pl.ds(j * PC, PC)],
                wg.at[j, y, x, c, pl.ds(pl.multiple_of(z * R, R), R), :],
                lsem.at[8 + j],
            )

        def own_bias():
            return pltpu.make_async_copy(b_own, bt.at[y, x, c, z], lsem.at[8 + panels])

        def gather_event(kind, panel):
            if not linked:
                if kind == "ready":
                    own_block(panel).wait()
            elif kind == "first":
                for t in slices(panel):
                    gather_first(t)
            elif kind == "second":
                for t in slices(panel):
                    gather_wait(t, 0)
                own_block(panel).wait()
                if panel == 0:
                    own_bias().wait()
                for t in slices(panel):
                    gather_send(t, 1)
            elif kind == "third":
                for t in slices(panel):
                    gather_wait(t, 1)
                for t in slices(panel):
                    gather_send(t, 2)
                for t in slices(panel):
                    core_send(t, False)
            elif kind == "pass":
                for t in slices(panel):
                    gather_wait(t, 2)
                for t in slices(panel):
                    core_send(t, True)
            elif kind == "ready":
                for t in slices(panel):
                    core_wait(t)

        load_n = lambda ref: pltpu.make_async_copy(n_hbm, ref, lsem.at[9 + panels])
        load_f = pltpu.make_async_copy(f_hbm, fg, lsem.at[10 + panels])

        def count_phase(nb, low, *digits):
            load_n(nb).start()
            peers = [me.peer(d, o) for d in "cxyz" for o in me.offsets(d) if linked]
            for p in peers:
                pl.semaphore_signal(
                    pltpu.get_barrier_semaphore(), inc=1,
                    device_id=p, device_id_type=MESH,
                )
            for j in range(panels):
                own_block(j).start()
            if linked:
                bias = b_in[...].astype(F32)
                bias = jnp.concatenate([bias, jnp.zeros((1, 128 - R), F32)], axis=1)
                bias = jnp.broadcast_to(bias, (8, 128))
                b_own[...] = pltpu.roll(bias, me.lane(R), 1)
                own_bias().start()
                pl.semaphore_wait(pltpu.get_barrier_semaphore(), len(peers))
            gather_event("first", 0)
            gather_event("first", 3)
            load_f.start()
            load_n(nb).wait()

            @pl.loop(0, chunks)
            def _(q):
                r = pl.ds(pl.multiple_of(q * 128, 128), 128)
                ids = nb[r, :]
                degree = jnp.sum((ids >= 0).astype(F32), axis=1, keepdims=True)
                fac[r, :] = jnp.broadcast_to(1.0 / (degree + 1.0), (128, 128))
                ids = ids.T
                high = ids >> (LOW.bit_length() - 1)
                digit = jnp.left_shift(jnp.ones_like(ids), (high & 3) * 8)
                low[:, r] = ids & (LOW - 1)
                for k, ref in enumerate(digits):
                    ref[:, r] = jnp.where(high >> 2 == k, digit, 0)

            gather_event("first", 1)
            place_in = lax.broadcasted_iota(I32, (LOW, 128), 0)
            lane = lax.broadcasted_iota(I32, (LOW, 128), 1)

            @pl.loop(0, chunks)
            def _(q):
                col = pl.ds(pl.multiple_of(q * 128, 128), 128)

                def step(s, carry):
                    some = pl.ds(pl.multiple_of(s * UNROLL, UNROLL), UNROLL)
                    lo, add = low[some, col], [ref[some, col] for ref in digits]
                    for k in range(UNROLL):
                        hit = lo[k : k + 1] == place_in
                        carry = tuple(
                            total + jnp.where(hit, a[k : k + 1], 0)
                            for total, a in zip(carry, add)
                        )
                    return carry

                zero = (jnp.zeros((LOW, 128), I32),) * len(digits)
                totals = lax.fori_loop(0, SLOTS // UNROLL, step, zero)
                cl, place = q // 8, q % 8
                to = pl.ds(pl.multiple_of(place * 128, 128), 128)
                for b in range(CLUSTER // LOW):
                    count = ((totals[b // 4] >> (8 * (b % 4))) & 255).astype(F32)
                    self_at = place * 128 - b * LOW
                    count = count + jnp.where(place_in - lane == self_at, 2.0, 0.0)
                    a2t[cl, pl.ds(b * LOW, LOW), to] = count.astype(BF16)
                for at, kind, panel in COUNT_EVENTS:
                    pl.when(q == at)(lambda k=kind, p=panel: gather_event(k, p))

        pl.run_scoped(
            count_phase,
            pltpu.VMEM((nodes, SLOTS), I32),
            *[pltpu.VMEM((SLOTS, nodes), I32)] * (1 + CLUSTER // LOW // 4),
        )
        load_f.wait()

        @pl.loop(0, clusters * 4)
        def _(s):
            cl, i, j = s // 4, (s // 2) % 2, s % 2
            r = pl.ds(pl.multiple_of(cl * CLUSTER + i * 512, 512), 512)
            k = pl.ds(pl.multiple_of(cl * CLUSTER, CLUSTER), CLUSTER)
            col = pl.ds(pl.multiple_of(j * half_rows, half_rows), half_rows)
            links = a2t[cl, :, pl.ds(pl.multiple_of(i * 512, 512), 512)]
            total = dot(links, fg[k, col], TN)
            scale = jnp.concatenate([fac[r, :]] * (half_rows // 128), axis=1)
            mixed[r, col] = (scale * total).astype(BF16)
            for at, kind, panel in MIX_EVENTS:
                pl.when(s == at)(lambda k=kind, p=panel: gather_event(k, p))

        half_y = Y // 2
        y_half = y // half_y

        def half_of(hh):
            if isinstance(hh, int):
                return y_half if hh else 1 - y_half
            return jnp.where(hh == 0, 1 - y_half, y_half)

        def part(pt, t, core, **at):
            ys, xs = at.get("y", ALL), at.get("x", ALL)
            if t == "bias":
                zs = pl.ds(at["z"], 1) if "z" in at else ALL
                return ptb.at[ys, xs, core, zs]
            zs = pl.ds(pl.multiple_of(at["z"] * R, R), R) if "z" in at else ALL
            return pt.at[t // 2, ys, xs, core, zs, pl.ds(t % 2 * HC, HC)]

        def scatter_path(t):
            return SCATTER[0] if t == "bias" else SCATTER[t]

        def landing(t, k):
            return stage[(len(SCATTER) if t == "bias" else t) * 3 + k]

        def scatter_send(pt, t, k, h=None):
            path = scatter_path(t)

            def make(o):
                at = fixed(path[:k])
                at[path[k]] = me.shifted(path[k], o)
                dst = landing(t, k).at[o - 1]
                if h is not None:
                    ys = pl.ds(half_of(h) * half_y, half_y)
                    at["y"] = ys
                    dst = dst.at[ys]
                return part(pt, t, c, **at), dst, me.peer(path[k], o)

            for o in me.offsets(path[k]):
                send(("scatter", t, k, o, h or 0), lambda o=o: make(o))

        def scatter_wait(t, k):
            path = scatter_path(t)
            for o in me.offsets(path[k]):
                ref = landing(t, k).at[o - 1]
                if t != "bias" and k == 0 and path[0] == "x":
                    for i in range(2):
                        ys = pl.ds(half_of(i) * half_y, half_y)
                        arrived(("scatter", t, k, o, i), ref.at[ys])
                else:
                    arrived(("scatter", t, k, o, 0), ref)

        def over_rows(shape, action):
            lead, high = shape[:-2], shape[-2]
            step = min(high, 64)

            def walk(index):
                if len(index) < len(lead):
                    if lead[len(index)] == 1:
                        walk(index + (0,))
                    else:
                        pl.loop(0, lead[len(index)])(lambda k: walk(index + (k,)))
                elif high == step:
                    action(index + (pl.ds(0, step),))
                else:
                    pl.loop(0, high // step)(
                        lambda k: action(
                            index + (pl.ds(pl.multiple_of(k * step, step), step),)
                        )
                    )

            walk(())

        def scatter_add(pt, t, k):
            path = scatter_path(t)
            mine = part(pt, t, c, **fixed(path[: k + 1]))
            others = [landing(t, k).at[o - 1] for o in me.offsets(path[k])]
            if t == "bias":
                total = mine[...]
                for other in others:
                    total = total + other[...]
                if k < 2:
                    mine[...] = total
                else:
                    gb_out[...] = total.reshape(8, 128)
                return

            def piece(at):
                total = mine[at].astype(F32)
                for other in others:
                    total = total + other[at].astype(F32)
                if k < 2:
                    mine[at] = total.astype(BF16)
                else:
                    gw_out[at[0], pl.ds(t * HC, HC)] = total

            over_rows(mine.shape, piece)

        def swap(pt, s):
            j, hh = s // 2, s % 2
            ys = pl.ds(half_of(hh) * half_y, half_y)
            i = sems["swap", 0] + s
            return pltpu.make_async_remote_copy(
                src_ref=pt.at[j, ys, :, 1 - c], dst_ref=cr.at[j, ys],
                send_sem=ssem.at[i], recv_sem=rsem.at[i],
                device_id=me.peer("c", 1), device_id_type=MESH,
            )

        def core_sum(pt, s):
            swap(pt, s).wait_recv()
            ys = pl.ds(half_of(s % 2) * half_y, half_y)
            mine, other = pt.at[s // 2, ys, :, c], cr.at[s // 2, ys]

            def piece(at):
                mine[at] = (mine[at].astype(F32) + other[at].astype(F32)).astype(BF16)

            over_rows(mine.shape, piece)

        def first_sends(pt, s):
            j, hh = s // 2, s % 2
            for t in (2 * j, 2 * j + 1):
                if scatter_path(t)[0] == "x":
                    scatter_send(pt, t, 0, hh)
                elif hh == (0 if Y == 2 else 1):
                    scatter_send(pt, t, 0)

        def scatter_event(pt, k, j):
            ts = (2 * j, 2 * j + 1) + (("bias",) if j == panels - 1 else ())
            for t in ts:
                scatter_wait(t, k - 1)
                scatter_add(pt, t, k - 1)
                if k < 3:
                    scatter_send(pt, t, k)

        def store_part(pt, s):
            j, hh = s // 2, s % 2
            ys = pl.ds(half_of(hh) * half_y, half_y)
            return pltpu.make_async_copy(
                pt.at[j, ys],
                gw_out.at[ys, :, :, :, pl.ds(pl.multiple_of(j * PC, PC), PC)],
                lsem.at[12 + panels + s],
            )

        def panel_phase(pt, acc_a, acc_b, go, ac):
            def tile_rows(i):
                return pl.ds(pl.multiple_of(i * TM, TM), TM)

            def block(hbm, j, i):
                return hbm.at[tile_rows(i), pl.ds(pl.multiple_of(j * PC, PC), PC)]

            def load_g(j, i):
                return pltpu.make_async_copy(block(g_hbm, j, i), go.at[i], lsem.at[i])

            def store_act(j, i):
                return pltpu.make_async_copy(
                    ac.at[i], block(act_hbm, j, i), lsem.at[4 + i]
                )

            def product(j, i):
                panel = wg[j].reshape(width, PC)
                return dot(mixed[tile_rows(i), :], panel, NN)

            def finish(acc, j, i):
                r = tile_rows(i)
                col = pl.ds(pl.multiple_of(j * PC, PC), PC)
                v = acc[...] + brow[0:1, col]
                u = v * v
                h = 0.5 + 0.5 * jnp.tanh(v * (ALPHA + BETA * u))
                a = v * h
                d = h + (a * (1.0 - h)) * (2 * ALPHA + (6 * BETA) * u)
                g = go[i].astype(F32) * d
                ac[i] = a.astype(BF16)
                fg[r, col] = g.astype(BF16)
                gbacc[:, col] += jnp.sum(g.reshape(TM // 8, 8, PC), axis=0)

            def weight_tile(j, hh):
                h = half_of(hh)
                rows_ = pl.ds(pl.multiple_of(h * half_rows, half_rows), half_rows)
                col = pl.ds(pl.multiple_of(j * PC, PC), PC)
                total = dot(mixed[:, rows_], fg[:, col], TN).astype(BF16)
                pt[j, pl.ds(h * half_y, half_y)] = total.reshape(half_y, X, 2, SR, PC)

            def leave(j, hh):
                if linked:
                    swap(pt, 2 * j + hh).start()
                else:
                    store_part(pt, 2 * j + hh).start()

            def events(step):
                for at, kind, panel in PANEL_GATHER:
                    pl.when(step == at)(lambda k=kind, p=panel: gather_event(k, p))
                if not linked:
                    return
                for at, k, panel in PANEL_SCATTER:
                    pl.when(step == at)(lambda k=k, p=panel: scatter_event(pt, k, p))

            def core_step(e, when):
                if not linked:
                    return

                @pl.when(when)
                def _():
                    core_sum(pt, e)
                    for fixed_e in range(2 * panels - 1):
                        pl.when(e == fixed_e)(lambda k=fixed_e: first_sends(pt, k))

            def send_bias():
                for d in range(n_dev):
                    col = pl.ds(d * R // 128 * 128, 128)
                    at = (d // (X * 2 * S), d // (2 * S) % X, d // S % 2, d % S)
                    ptb[at] = gbacc[:, col]
                send(
                    ("swap", "bias"),
                    lambda: (ptb.at[:, :, 1 - c], crb, me.peer("c", 1)),
                )

            def sum_bias():
                arrived(("swap", "bias"), crb)
                mine = ptb.at[:, :, c]
                mine[...] = mine[...] + crb[...]
                scatter_send(pt, "bias", 0)

            def panel(j):
                final = panels - 1

                @pl.loop(0, per_panel // 2)
                def _(h):
                    for k, acc, other in ((0, acc_a, acc_b), (1, acc_b, acc_a)):
                        i = 2 * h + k
                        load_g(j, i).wait()
                        pl.when(j > 0)(lambda i=i: store_act(j - 1, i).wait())
                    for k, acc, other in ((0, acc_a, acc_b), (1, acc_b, acc_a)):
                        i = 2 * h + k
                        n = jnp.minimum(j * per_panel + i + 1, tiles - 1)
                        other[...] = product(n // per_panel, n % per_panel)
                        finish(acc, j, i)
                    for k in range(2):
                        i = 2 * h + k
                        store_act(j, i).start()
                        pl.when(j < final)(lambda i=i: load_g(j + 1, i).start())
                    core_step(2 * j - 1, (h == 0) & (j > 0))
                    events(4 * j + h)

                @pl.loop(0, 2)
                def _(hh):
                    if linked:
                        pl.when((j == final) & (hh == 0))(send_bias)
                    weight_tile(j, hh)
                    leave(j, hh)
                    if linked:
                        pl.when((j == final) & (hh == 1))(sum_bias)
                    core_step(2 * j, hh == 1)
                    events(4 * j + 2 + hh)

            for i in range(per_panel):
                load_g(0, i).start()
            gather_event("ready", 0)
            p = 128 // R
            if not linked:
                brow[...] = b_in[...]
            for k in range(width // 128 if linked else 0):
                tile = jnp.zeros((8, 128), F32)
                for d in range(k * p, (k + 1) * p):
                    tile = tile + bt[d // (X * 2 * S), d // (2 * S) % X, d // S % 2, d % S]
                brow[:, pl.ds(k * 128, 128)] = tile
            gbacc[...] = jnp.zeros_like(gbacc)
            acc_a[...] = product(0, 0)
            pl.loop(0, panels)(panel)
            for i in range(per_panel):
                store_act(panels - 1, i).wait()

        def back_phase(pt):
            steps = nodes // BM

            @pl.loop(0, steps)
            def _(s):
                r = pl.ds(pl.multiple_of(s * BM, BM), BM)
                total = None
                for j in range(panels):
                    rhs = wg[j].reshape(width, PC)
                    term = dot(fg[r, pl.ds(j * PC, PC)], rhs, NT)
                    total = term if total is None else total + term
                scale = jnp.concatenate([fac[r, :]] * (width // 128), axis=1)
                fg[r, :] = (scale * total).astype(BF16)
                if not linked:
                    return

                @pl.when(s == 0)
                def _():
                    core_sum(pt, 2 * panels - 1)
                    first_sends(pt, 2 * panels - 1)

                for at, k, panel in BACK_SCATTER:
                    pl.when(s == at)(lambda k=k, p=panel: scatter_event(pt, k, p))

            if linked:
                scatter_event(pt, 3, panels - 1)
                for s in range(2 * panels):
                    swap(pt, s).wait_send()
                for name, make in started.items():
                    remote(name, *make()).wait_send()
            else:
                for s in range(2 * panels):
                    store_part(pt, s).wait()
                gb_out[...] = gbacc[...]

        def with_parts(pt):
            pl.run_scoped(
                lambda *refs: panel_phase(pt, *refs),
                *[pltpu.VMEM((TM, PC), F32)] * 2,
                *[pltpu.VMEM((per_panel, TM, PC), BF16)] * 2,
            )
            back_phase(pt)

        pl.run_scoped(with_parts, pltpu.VMEM((panels, Y, X, 2, SR, PC), BF16))

    away = pl.BlockSpec(memory_space=pltpu.HBM)
    here = pl.BlockSpec(memory_space=pltpu.VMEM)
    scratch = [
        pltpu.VMEM((nodes, width), BF16),
        pltpu.VMEM((panels, Y, X, 2, SR, PC), BF16),
        pltpu.VMEM((nodes, 128), F32),
        pltpu.VMEM((8, 128), F32),
        pltpu.VMEM((Y, X, 2, S, 8, 128), F32),
        pltpu.VMEM((8, width), F32),
        pltpu.VMEM((8, width), F32),
        pltpu.VMEM((panels, Y, X, SR, PC), BF16),
        pltpu.VMEM((Y, X, S, 8, 128), F32),
        pltpu.VMEM((Y, X, 2, S, 8, 128), F32),
        *stage_shapes(),
        pltpu.SemaphoreType.DMA((n_sems,)),
        pltpu.SemaphoreType.DMA((n_sems,)),
        pltpu.SemaphoreType.DMA((12 + 3 * panels,)),
    ]
    if not linked:
        for k in (3, 4, 7, 8, 9, *range(10, 10 + n_stage)):
            scratch[k] = pltpu.VMEM((8, 128), F32)
        scratch[-3] = scratch[-2] = pltpu.SemaphoreType.DMA((1,))
    return pl.pallas_call(
        kernel,
        out_shape=(
            jax.ShapeDtypeStruct((nodes, width), BF16),
            pltpu.VMEM((nodes, width), BF16),
            pltpu.VMEM((clusters, CLUSTER, CLUSTER), BF16),
            pltpu.VMEM((R, width), F32)
            if linked
            else jax.ShapeDtypeStruct((Y, X, 2, SR, width), BF16),
            pltpu.VMEM((8, 128 if linked else width), F32),
        ),
        in_specs=[away] * 3 + [here, away],
        out_specs=(away, here, here, here if linked else away, here),
        scratch_shapes=scratch,
        compiler_params=pltpu.CompilerParams(
            collective_id=0 if linked else None,
            has_side_effects=True,
            vmem_limit_bytes=48 * 2**20,
        ),
        name="layer",
    )


def make_last(dp_size, shard_size, rows, width, nodes):
    clusters = nodes // CLUSTER
    per_cluster = width // PC
    steps = clusters * per_cluster
    part_rows = nodes // steps
    linked = linkable(rows)

    def kernel(links, spread, act_in, gw_in, gb_in, out, act_out, gw_out, gb_out, held, tiles, sem):
        def inward(k):
            part = act_in.at[pl.ds(pl.multiple_of(k * part_rows, part_rows), part_rows)]
            return pltpu.make_async_copy(part, held.at[k], sem.at[k])

        def outward(k):
            part = act_out.at[pl.ds(pl.multiple_of(k * part_rows, part_rows), part_rows)]
            return pltpu.make_async_copy(held.at[k], part, sem.at[steps + k])

        def place(k):
            return (
                pl.ds(pl.multiple_of(k // per_cluster * CLUSTER, CLUSTER), CLUSTER),
                pl.ds(pl.multiple_of(k % per_cluster * PC, PC), PC),
            )

        def store(k):
            return pltpu.make_async_copy(
                tiles.at[k % 2], out.at[place(k)], sem.at[2 * steps + k % 2]
            )

        carry = pltpu.make_async_copy(gw_in, gw_out, sem.at[2 * steps + 2])
        @pl.loop(0, steps)
        def _(k):
            inward(k).start()

        if linked:
            carry.start()
            me = Place(dp_size, shard_size)
            total = jnp.sum(gb_in[...], axis=0, keepdims=True)
            total = jnp.broadcast_to(total, (8, 128))
            gb_out[...] = pltpu.roll(total, (128 - me.lane(rows)) % 128, 1)[0:1, :rows]

        @pl.loop(0, steps)
        def _(k):
            pl.when(k >= 2)(lambda: store(k - 2).wait())
            tiles[k % 2] = dot(links[k // per_cluster], spread[place(k)], NN)
            store(k).start()
            inward(k).wait()
            outward(k).start()

        @pl.loop(0, steps)
        def _(k):
            outward(k).wait()

        for k in (steps - 2, steps - 1):
            store(k).wait()
        if linked:
            carry.wait()

    away = pl.BlockSpec(memory_space=pltpu.HBM)
    here = pl.BlockSpec(memory_space=pltpu.VMEM)
    return pl.pallas_call(
        kernel,
        out_shape=(
            jax.ShapeDtypeStruct((nodes, width), F32),
            jax.ShapeDtypeStruct((nodes, width), BF16),
            jax.ShapeDtypeStruct((rows, width), F32),
            jax.ShapeDtypeStruct((1, rows), F32),
        ),
        in_specs=[here, here, away, here, here],
        out_specs=(away, away, away, here),
        scratch_shapes=[
            pltpu.VMEM((steps, part_rows, width), BF16),
            pltpu.VMEM((2, CLUSTER, PC), F32),
            pltpu.SemaphoreType.DMA((2 * steps + 3,)),
        ],
        compiler_params=pltpu.CompilerParams(vmem_limit_bytes=14 * 2**20),
        name="features",
    )


def solution(mesh):
    dp_size, shard_size = mesh.shape["dp"], mesh.shape["shard"]

    def keep(array):
        return pltpu.with_memory_space_constraint(array, pltpu.VMEM)

    def leave(array):
        return pltpu.with_memory_space_constraint(array, pltpu.HBM)

    def on_device(features, neighbors, weight, bias_terms, grad_out):
        nodes, width = features.shape
        rows = weight.shape[0]
        layer = make_kernel(dp_size, shard_size, rows, width, nodes)
        last = make_last(dp_size, shard_size, rows, width, nodes)
        if linkable(rows):
            act, spread, links, grad_weight, bias_sums = layer(
                features, neighbors, weight, bias_terms.reshape(1, rows), grad_out
            )
            grad_features, output, grad_weight, grad_bias = last(
                keep(links), keep(spread), leave(act), keep(grad_weight), keep(bias_sums)
            )
            return output, grad_features, grad_weight, grad_bias.reshape(rows)
        both = ("dp", "shard")
        full = lax.all_gather(weight, both, axis=0, tiled=True)
        bias = lax.all_gather(bias_terms, both, axis=0, tiled=True).astype(F32)
        act, spread, links, parts, bias_sums = layer(
            features,
            neighbors,
            full.reshape(dp_size // 4, 2, 2, shard_size * rows, width),
            jnp.broadcast_to(bias, (8, width)),
            grad_out,
        )
        grad_features, output, *_ = last(
            keep(links),
            keep(spread),
            leave(act),
            jnp.zeros((rows, width), F32),
            jnp.zeros((8, 128), F32),
        )
        parts = parts.reshape(width, width).astype(F32)
        bias_sums = jnp.sum(bias_sums, axis=0)
        return (
            output,
            grad_features,
            lax.psum_scatter(parts, both, scatter_dimension=0, tiled=True),
            lax.psum_scatter(bias_sums, both, scatter_dimension=0, tiled=True),
        )

    split = P(("dp", "shard"), None)
    flat = P(("dp", "shard"))
    return jax.shard_map(
        on_device,
        mesh=mesh,
        in_specs=(split, split, split, flat, split),
        out_specs=(split, split, split, flat),
        check_vma=False,
    )
```

```python
import jax
import jax.numpy as jnp
from jax import lax
from jax.experimental import pallas as pl
from jax.experimental.pallas import tpu as pltpu
from jax.sharding import PartitionSpec as P

F32, BF16, I32 = jnp.float32, jnp.bfloat16, jnp.int32
MESH = pl.DeviceIdType.MESH
CLUSTER = 1024
SLOTS = 128
UNROLL = 32
LOW = 64
PC = 512
HC = 256
ALPHA = 0.7978845608028654
BETA = ALPHA * 0.044715
NN = (((1,), (0,)), ((), ()))
TN = (((0,), (0,)), ((), ()))
NT = (((1,), (1,)), ((), ()))
ALL = slice(None)

GATHER = ("zxy", "zyx", "zxy", "zyx", "zxy", "zyx", "xzy", "yzx")
SCATTER = ("yzx", "xzy", "yxz", "xyz", "yxz", "xyz", "yxz", "xyz")
COUNT_EVENTS = (
    (4, "second", 0),
    (6, "first", 2),
    (8, "third", 0),
    (8, "second", 1),
    (12, "second", 3),
    (12, "second", 2),
)
MIX_EVENTS = (
    (0, "third", 1),
    (0, "pass", 0),
    (3, "third", 2),
    (7, "third", 3),
    (7, "pass", 1),
)
PANEL_GATHER = (
    (0, "ready", 1),
    (3, "pass", 2),
    (4, "ready", 2),
    (6, "pass", 3),
    (8, "ready", 3),
)
PANEL_SCATTER = ((9, 1, 0), (13, 1, 1), (15, 2, 0), (17, 2, 1))
BACK_SCATTER = (
    (0, 3, 0),
    (0, 1, 2),
    (2, 3, 1),
    (3, 2, 2),
    (4, 1, 3),
    (6, 3, 2),
    (6, 2, 3),
)


def dot(a, b, dims):
    return lax.dot_general(a, b, dims, preferred_element_type=F32)


class Place:
    def __init__(self, dp_size, shard_size):
        dp, self.z = lax.axis_index("dp"), lax.axis_index("shard")
        self.dp = dp
        self.c, self.x, self.y = dp % 2, (dp // 2) % 2, dp // 4
        self.size = {"c": 2, "x": 2, "y": dp_size // 4, "z": shard_size}

    def at(self, dim):
        return {"c": self.c, "x": self.x, "y": self.y, "z": self.z}[dim]

    def shifted(self, dim, offset):
        size = self.size[dim]
        return lax.rem(self.at(dim) + (offset + size), size)

    def peer(self, dim, offset):
        other = self.shifted(dim, offset)
        if dim == "z":
            return (self.dp, other)
        step = {"c": 1, "x": 2, "y": 4}[dim]
        return (self.dp + step * (other - self.at(dim)), self.z)

    def lane(self, rows):
        return (self.dp * self.size["z"] + self.z) * rows % 128

    def offsets(self, dim):
        return range(1, self.size[dim])


class Sems:
    def __init__(self):
        self.index = {}

    def __getitem__(self, name):
        return self.index.setdefault(name, len(self.index))


def sem_names(sizes):
    sems = Sems()
    for t in list(range(len(GATHER))) + ["bias"]:
        path = GATHER[0] if t == "bias" else GATHER[t]
        for k in range(3):
            for o in range(1, sizes[path[k]]):
                sems["gather", t, k, o]
        sems["core", t, 0]
        for o in range(1, sizes[path[2]]):
            sems["core", t, o]
    for t in list(range(len(SCATTER))) + ["bias"]:
        path = SCATTER[0] if t == "bias" else SCATTER[t]
        for k in range(3):
            for o in range(1, sizes[path[k]]):
                sems["scatter", t, k, o]
    sems["swap", "bias"]
    for j in range(len(SCATTER) // 2):
        sems["swap", j]
    return sems


def linkable(rows):
    return rows % 16 == 0


def make_kernel(dp_size, shard_size, rows, width, nodes):
    sizes = {"c": 2, "x": 2, "y": dp_size // 4, "z": shard_size}
    Y, X, S, R = sizes["y"], 2, shard_size, rows
    SR = S * R
    n_dev = dp_size * shard_size
    panels = width // PC
    half_rows = width // 2
    clusters = nodes // CLUSTER
    sems = sem_names(sizes)
    n_sems = len(sems.index)
    chunks = nodes // 128
    TM = 512
    tiles = (nodes // TM) * panels
    per_panel = nodes // TM
    BM = 256

    def stage_shape(path, k):
        n = sizes[path[k]] - 1
        left = path[k + 1 :]
        lead = tuple(sizes[d] for d in "yx" if d in left)
        return (n,) + lead, ("z" in left)

    def stage_shapes():
        out = []
        for t in range(len(SCATTER)):
            for k in range(3):
                lead, z = stage_shape(SCATTER[t], k)
                out.append(pltpu.VMEM(lead + (SR if z else R, HC), BF16))
        for k in range(3):
            lead, z = stage_shape(SCATTER[0], k)
            out.append(pltpu.VMEM(lead + (S if z else 1, 8, 128), F32))
        return out

    n_stage = 3 * (len(SCATTER) + 1)
    linked = linkable(rows)

    def kernel(
        f_hbm, n_hbm, w_hbm, b_in, g_hbm,
        act_hbm, fg, a2t, gw_out, gb_out,
        mixed, wg, fac, b_own, bt, brow, gbacc, cr, crb, ptb, *rest,
    ):
        stage = rest[:n_stage]
        ssem, rsem, lsem = rest[n_stage:]
        me = Place(dp_size, shard_size)
        c, x, y, z = me.c, me.x, me.y, me.z
        started = {}

        def remote(name, src, dst, device):
            i = sems[name]
            return pltpu.make_async_remote_copy(
                src_ref=src, dst_ref=dst, send_sem=ssem.at[i], recv_sem=rsem.at[i],
                device_id=device, device_id_type=MESH,
            )

        def send(name, make):
            remote(name, *make()).start()
            started[name] = make

        def arrived(name, ref):
            remote(name, ref, ref, me.peer("c", 1)).wait_recv()

        def view(t, core, **at):
            ys, xs = at.get("y", ALL), at.get("x", ALL)
            if t == "bias":
                zs = pl.ds(at["z"], 1) if "z" in at else ALL
                return bt.at[ys, xs, core, zs]
            zs = pl.ds(pl.multiple_of(at["z"] * R, R), R) if "z" in at else ALL
            return wg.at[t // 2, ys, xs, core, zs, pl.ds(t % 2 * HC, HC)]

        own = {"x": x, "y": y, "z": z}

        def fixed(dims):
            return {d: own[d] for d in dims}

        def gather_path(t):
            return GATHER[0] if t == "bias" else GATHER[t]

        def gather_first(t):
            path = gather_path(t)

            def make(o):
                if t == "bias":
                    return b_own, bt.at[y, x, c, z], me.peer(path[0], o)
                src = w_hbm.at[:, pl.ds(t * HC, HC)]
                return src, view(t, c, **fixed("xyz")), me.peer(path[0], o)

            for o in me.offsets(path[0]):
                send(("gather", t, 0, o), lambda o=o: make(o))

        def gather_wait(t, k):
            path = gather_path(t)
            for o in me.offsets(path[k]):
                at = fixed(path[k:])
                at[path[k]] = me.shifted(path[k], -o)
                arrived(("gather", t, k, o), view(t, c, **at))

        def gather_send(t, k):
            path = gather_path(t)

            def make(o):
                ref = view(t, c, **fixed(path[k:]))
                return ref, ref, me.peer(path[k], o)

            for o in me.offsets(path[k]):
                send(("gather", t, k, o), lambda o=o: make(o))

        def core_send(t, late):
            path = gather_path(t)

            def make(o):
                at = {path[2]: me.shifted(path[2], -o)} if o else fixed(path[2:])
                ref = view(t, c, **at)
                return ref, ref, me.peer("c", 1)

            for o in me.offsets(path[2]) if late else (0,):
                send(("core", t, o), lambda o=o: make(o))

        def core_wait(t):
            path = gather_path(t)
            arrived(("core", t, 0), view(t, 1 - c, **fixed(path[2:])))
            for o in me.offsets(path[2]):
                arrived(
                    ("core", t, o),
                    view(t, 1 - c, **{path[2]: me.shifted(path[2], -o)}),
                )

        def slices(panel):
            return (2 * panel, 2 * panel + 1) + (("bias",) if panel == 0 else ())

        def own_block(j):
            if not linked:
                return pltpu.make_async_copy(
                    w_hbm.at[:, :, :, :, pl.ds(j * PC, PC)], wg.at[j], lsem.at[8 + j]
                )
            return pltpu.make_async_copy(
                w_hbm.at[:, pl.ds(j * PC, PC)],
                wg.at[j, y, x, c, pl.ds(pl.multiple_of(z * R, R), R), :],
                lsem.at[8 + j],
            )

        def own_bias():
            return pltpu.make_async_copy(b_own, bt.at[y, x, c, z], lsem.at[8 + panels])

        def gather_event(kind, panel):
            if not linked:
                if kind == "ready":
                    own_block(panel).wait()
            elif kind == "first":
                for t in slices(panel):
                    gather_first(t)
            elif kind == "second":
                for t in slices(panel):
                    gather_wait(t, 0)
                own_block(panel).wait()
                if panel == 0:
                    own_bias().wait()
                for t in slices(panel):
                    gather_send(t, 1)
            elif kind == "third":
                for t in slices(panel):
                    gather_wait(t, 1)
                for t in slices(panel):
                    gather_send(t, 2)
                for t in slices(panel):
                    core_send(t, False)
            elif kind == "pass":
                for t in slices(panel):
                    gather_wait(t, 2)
                for t in slices(panel):
                    core_send(t, True)
            elif kind == "ready":
                for t in slices(panel):
                    core_wait(t)

        load_n = lambda ref: pltpu.make_async_copy(n_hbm, ref, lsem.at[9 + panels])
        load_f = pltpu.make_async_copy(f_hbm, fg, lsem.at[10 + panels])

        def count_phase(nb, low, *digits):
            load_n(nb).start()
            peers = [me.peer(d, o) for d in "cxyz" for o in me.offsets(d) if linked]
            for p in peers:
                pl.semaphore_signal(
                    pltpu.get_barrier_semaphore(), inc=1,
                    device_id=p, device_id_type=MESH,
                )
            for j in range(panels):
                own_block(j).start()
            if linked:
                bias = b_in[...].astype(F32)
                bias = jnp.concatenate([bias, jnp.zeros((1, 128 - R), F32)], axis=1)
                bias = jnp.broadcast_to(bias, (8, 128))
                b_own[...] = pltpu.roll(bias, me.lane(R), 1)
                own_bias().start()
                pl.semaphore_wait(pltpu.get_barrier_semaphore(), len(peers))
            gather_event("first", 0)
            gather_event("first", 3)
            load_f.start()
            load_n(nb).wait()

            @pl.loop(0, chunks)
            def _(q):
                r = pl.ds(pl.multiple_of(q * 128, 128), 128)
                ids = nb[r, :]
                degree = jnp.sum((ids >= 0).astype(F32), axis=1, keepdims=True)
                fac[r, :] = jnp.broadcast_to(1.0 / (degree + 1.0), (128, 128))
                ids = ids.T
                high = ids >> (LOW.bit_length() - 1)
                digit = jnp.left_shift(jnp.ones_like(ids), (high & 3) * 8)
                low[:, r] = ids & (LOW - 1)
                for k, ref in enumerate(digits):
                    ref[:, r] = jnp.where(high >> 2 == k, digit, 0)

            gather_event("first", 1)
            place_in = lax.broadcasted_iota(I32, (LOW, 128), 0)
            lane = lax.broadcasted_iota(I32, (LOW, 128), 1)

            @pl.loop(0, chunks)
            def _(q):
                col = pl.ds(pl.multiple_of(q * 128, 128), 128)

                def step(s, carry):
                    some = pl.ds(pl.multiple_of(s * UNROLL, UNROLL), UNROLL)
                    lo, add = low[some, col], [ref[some, col] for ref in digits]
                    for k in range(UNROLL):
                        hit = lo[k : k + 1] == place_in
                        carry = tuple(
                            total + jnp.where(hit, a[k : k + 1], 0)
                            for total, a in zip(carry, add)
                        )
                    return carry

                zero = (jnp.zeros((LOW, 128), I32),) * len(digits)
                totals = lax.fori_loop(0, SLOTS // UNROLL, step, zero)
                cl, place = q // 8, q % 8
                to = pl.ds(pl.multiple_of(place * 128, 128), 128)
                for b in range(CLUSTER // LOW):
                    count = ((totals[b // 4] >> (8 * (b % 4))) & 255).astype(F32)
                    self_at = place * 128 - b * LOW
                    count = count + jnp.where(place_in - lane == self_at, 2.0, 0.0)
                    a2t[cl, pl.ds(b * LOW, LOW), to] = count.astype(BF16)
                for at, kind, panel in COUNT_EVENTS:
                    pl.when(q == at)(lambda k=kind, p=panel: gather_event(k, p))

        pl.run_scoped(
            count_phase,
            pltpu.VMEM((nodes, SLOTS), I32),
            *[pltpu.VMEM((SLOTS, nodes), I32)] * (1 + CLUSTER // LOW // 4),
        )
        load_f.wait()

        @pl.loop(0, clusters * 4)
        def _(s):
            cl, i, j = s // 4, (s // 2) % 2, s % 2
            r = pl.ds(pl.multiple_of(cl * CLUSTER + i * 512, 512), 512)
            k = pl.ds(pl.multiple_of(cl * CLUSTER, CLUSTER), CLUSTER)
            col = pl.ds(pl.multiple_of(j * half_rows, half_rows), half_rows)
            links = a2t[cl, :, pl.ds(pl.multiple_of(i * 512, 512), 512)]
            total = dot(links, fg[k, col], TN)
            scale = jnp.concatenate([fac[r, :]] * (half_rows // 128), axis=1)
            mixed[r, col] = (scale * total).astype(BF16)
            for at, kind, panel in MIX_EVENTS:
                pl.when(s == at)(lambda k=kind, p=panel: gather_event(k, p))

        def part(pt, t, **at):
            ys, xs = at.get("y", ALL), at.get("x", ALL)
            if t == "bias":
                zs = pl.ds(at["z"], 1) if "z" in at else ALL
                return ptb.at[ys, xs, c, zs]
            zs = pl.ds(pl.multiple_of(at["z"] * R, R), R) if "z" in at else ALL
            return pt.at[t // 2, ys, xs, zs, pl.ds(t % 2 * HC, HC)]

        def scatter_path(t):
            return SCATTER[0] if t == "bias" else SCATTER[t]

        def landing(t, k):
            return stage[(len(SCATTER) if t == "bias" else t) * 3 + k]

        def scatter_send(pt, t, k):
            path = scatter_path(t)

            def make(o):
                at = fixed(path[:k])
                at[path[k]] = me.shifted(path[k], o)
                return part(pt, t, **at), landing(t, k).at[o - 1], me.peer(path[k], o)

            for o in me.offsets(path[k]):
                send(("scatter", t, k, o), lambda o=o: make(o))

        def scatter_wait(t, k):
            for o in me.offsets(scatter_path(t)[k]):
                arrived(("scatter", t, k, o), landing(t, k).at[o - 1])

        def over_rows(shape, action):
            lead, high = shape[:-2], shape[-2]
            step = min(high, 64)

            def walk(index):
                if len(index) < len(lead):
                    if lead[len(index)] == 1:
                        walk(index + (0,))
                    else:
                        pl.loop(0, lead[len(index)])(lambda k: walk(index + (k,)))
                elif high == step:
                    action(index + (pl.ds(0, step),))
                else:
                    pl.loop(0, high // step)(
                        lambda k: action(
                            index + (pl.ds(pl.multiple_of(k * step, step), step),)
                        )
                    )

            walk(())

        def scatter_add(pt, t, k):
            path = scatter_path(t)
            mine = part(pt, t, **fixed(path[: k + 1]))
            others = [landing(t, k).at[o - 1] for o in me.offsets(path[k])]
            if t == "bias":
                total = mine[...]
                for other in others:
                    total = total + other[...]
                if k < 2:
                    mine[...] = total
                else:
                    gb_out[...] = total.reshape(8, 128)
                return

            def piece(at):
                total = mine[at].astype(F32)
                for other in others:
                    total = total + other[at].astype(F32)
                if k < 2:
                    mine[at] = total.astype(BF16)
                else:
                    gw_out[at[0], pl.ds(t * HC, HC)] = total

            over_rows(mine.shape, piece)

        def swap(po, j):
            i = sems["swap", 0] + j
            return pltpu.make_async_remote_copy(
                src_ref=po.at[j], dst_ref=cr.at[j],
                send_sem=ssem.at[i], recv_sem=rsem.at[i],
                device_id=me.peer("c", 1), device_id_type=MESH,
            )

        def scatter_event(pt, k, j):
            ts = (2 * j, 2 * j + 1) + (("bias",) if j == panels - 1 else ())
            for t in ts:
                scatter_wait(t, k - 1)
                scatter_add(pt, t, k - 1)
                if k < 3:
                    scatter_send(pt, t, k)

        def store_part(held, j, core, k):
            col = pl.ds(pl.multiple_of(j * PC, PC), PC)
            return pltpu.make_async_copy(
                held.at[j],
                gw_out.at[:, :, core, :, col],
                lsem.at[12 + (1 + k) * panels + j],
            )

        def panel_phase(pt, po, acc_a, acc_b, go, ac):
            def tile_rows(i):
                return pl.ds(pl.multiple_of(i * TM, TM), TM)

            def block(hbm, j, i):
                return hbm.at[tile_rows(i), pl.ds(pl.multiple_of(j * PC, PC), PC)]

            def load_g(j, i):
                return pltpu.make_async_copy(block(g_hbm, j, i), go.at[i], lsem.at[i])

            def store_act(j, i):
                return pltpu.make_async_copy(
                    ac.at[i], block(act_hbm, j, i), lsem.at[4 + i]
                )

            def product(j, i, cols):
                panel = wg[j, :, :, :, :, cols].reshape(width, HC)
                return dot(mixed[tile_rows(i), :], panel, NN)

            def finish(acc, j, i, cols):
                r = tile_rows(i)
                col = pl.ds(pl.multiple_of(j * PC + cols.start, HC), HC)
                v = acc[:, cols] + brow[0:1, col]
                u = v * v
                h = 0.5 + 0.5 * jnp.tanh(v * (ALPHA + BETA * u))
                a = v * h
                d = h + (a * (1.0 - h)) * (2 * ALPHA + (6 * BETA) * u)
                g = go[i, :, cols].astype(F32) * d
                ac[i, :, cols] = a.astype(BF16)
                fg[r, col] = g.astype(BF16)
                gbacc[:, col] += jnp.sum(g.reshape(TM // 8, 8, HC), axis=0)

            def weight_rows(j, core):
                lhs = [
                    mixed[:, pl.ds(pl.multiple_of((b * 2 + core) * SR, SR), SR)]
                    for b in range(Y * X)
                ]
                col = pl.ds(pl.multiple_of(j * PC, PC), PC)
                total = dot(jnp.concatenate(lhs, axis=1), fg[:, col], TN)
                return total.reshape(Y, X, SR, PC)

            def events(step):
                for at, kind, panel in PANEL_GATHER:
                    pl.when(step == at)(lambda k=kind, p=panel: gather_event(k, p))
                if not linked:
                    return
                for at, k, panel in PANEL_SCATTER:
                    pl.when(step == at)(lambda k=k, p=panel: scatter_event(pt, k, p))

            def send_bias():
                for d in range(n_dev):
                    col = pl.ds(d * R // 128 * 128, 128)
                    at = (d // (X * 2 * S), d // (2 * S) % X, d // S % 2, d % S)
                    ptb[at] = gbacc[:, col]
                send(
                    ("swap", "bias"),
                    lambda: (ptb.at[:, :, 1 - c], crb, me.peer("c", 1)),
                )

            def sum_bias():
                arrived(("swap", "bias"), crb)
                mine = ptb.at[:, :, c]
                mine[...] = mine[...] + crb[...]
                scatter_send(pt, "bias", 0)

            def pair(j, h):
                for k in range(2):
                    load_g(j, 2 * h + k).wait()
                    pl.when(j > 0)(lambda i=2 * h + k: store_act(j - 1, i).wait())
                for k, acc, other in ((0, acc_a, acc_b), (1, acc_b, acc_a)):
                    i = 2 * h + k
                    n = jnp.minimum(j * per_panel + i + 1, tiles - 1)
                    for q in range(PC // HC):
                        cols = pl.ds(q * HC, HC)
                        other[:, cols] = product(n // per_panel, n % per_panel, cols)
                        finish(acc, j, i, cols)
                for k in range(2):
                    i = 2 * h + k
                    store_act(j, i).start()
                    pl.when(j < panels - 1)(lambda i=i: load_g(j + 1, i).start())

            def own_rows(j):
                total = weight_rows(j, c)
                if linked:
                    swap(po, j).wait_recv()
                    total = total + cr[j].astype(F32)
                pt[j] = total.astype(BF16)
                if not linked:
                    store_part(pt, j, c, 0).start()
                    return
                for p in range(panels):

                    @pl.when(j == p)
                    def _():
                        for t in (2 * p, 2 * p + 1):
                            scatter_send(pt, t, 0)
                        if p == panels - 1:
                            sum_bias()

            def other_rows(j):
                po[j] = weight_rows(j, 1 - c).astype(BF16)
                if linked:
                    swap(po, j).start()
                    pl.when(j == panels - 1)(send_bias)
                else:
                    store_part(po, j, 1 - c, 1).start()

            def panel(j):
                @pl.loop(0, 2)
                def _(h):
                    pl.when(j < panels)(lambda: pair(j, h))
                    events(4 * j + 2 * h)
                    pl.when((h == 0) & (j > 0))(lambda: own_rows(j - 1))
                    pl.when((h == 1) & (j < panels))(lambda: other_rows(j))
                    events(4 * j + 2 * h + 1)

            for i in range(per_panel):
                load_g(0, i).start()
            gather_event("ready", 0)
            p = 128 // R
            if not linked:
                brow[...] = b_in[...]
            for k in range(width // 128 if linked else 0):
                tile = jnp.zeros((8, 128), F32)
                for d in range(k * p, (k + 1) * p):
                    tile = tile + bt[d // (X * 2 * S), d // (2 * S) % X, d // S % 2, d % S]
                brow[:, pl.ds(k * 128, 128)] = tile
            gbacc[...] = jnp.zeros_like(gbacc)
            for q in range(PC // HC):
                cols = pl.ds(q * HC, HC)
                acc_a[:, cols] = product(0, 0, cols)
            pl.loop(0, panels + 1)(panel)
            for i in range(per_panel):
                store_act(panels - 1, i).wait()

        def back_phase(pt, po):
            steps = nodes // BM

            @pl.loop(0, steps)
            def _(s):
                r = pl.ds(pl.multiple_of(s * BM, BM), BM)
                total = None
                for j in range(panels):
                    rhs = wg[j].reshape(width, PC)
                    term = dot(fg[r, pl.ds(j * PC, PC)], rhs, NT)
                    total = term if total is None else total + term
                scale = jnp.concatenate([fac[r, :]] * (width // 128), axis=1)
                fg[r, :] = (scale * total).astype(BF16)
                if not linked:
                    return

                for at, k, panel in BACK_SCATTER:
                    pl.when(s == at)(lambda k=k, p=panel: scatter_event(pt, k, p))

            if linked:
                scatter_event(pt, 3, panels - 1)
                for j in range(panels):
                    swap(po, j).wait_send()
                for name, make in started.items():
                    remote(name, *make()).wait_send()
            else:
                for j in range(panels):
                    store_part(pt, j, c, 0).wait()
                    store_part(po, j, 1 - c, 1).wait()
                gb_out[...] = gbacc[...]

        def with_parts(pt, po):
            pl.run_scoped(
                lambda *refs: panel_phase(pt, po, *refs),
                *[pltpu.VMEM((TM, PC), F32)] * 2,
                *[pltpu.VMEM((per_panel, TM, PC), BF16)] * 2,
            )
            back_phase(pt, po)

        pl.run_scoped(with_parts, *[pltpu.VMEM((panels, Y, X, SR, PC), BF16)] * 2)

    away = pl.BlockSpec(memory_space=pltpu.HBM)
    here = pl.BlockSpec(memory_space=pltpu.VMEM)
    scratch = [
        pltpu.VMEM((nodes, width), BF16),
        pltpu.VMEM((panels, Y, X, 2, SR, PC), BF16),
        pltpu.VMEM((nodes, 128), F32),
        pltpu.VMEM((8, 128), F32),
        pltpu.VMEM((Y, X, 2, S, 8, 128), F32),
        pltpu.VMEM((8, width), F32),
        pltpu.VMEM((8, width), F32),
        pltpu.VMEM((panels, Y, X, SR, PC), BF16),
        pltpu.VMEM((Y, X, S, 8, 128), F32),
        pltpu.VMEM((Y, X, 2, S, 8, 128), F32),
        *stage_shapes(),
        pltpu.SemaphoreType.DMA((n_sems,)),
        pltpu.SemaphoreType.DMA((n_sems,)),
        pltpu.SemaphoreType.DMA((12 + 3 * panels,)),
    ]
    if not linked:
        for k in (3, 4, 7, 8, 9, *range(10, 10 + n_stage)):
            scratch[k] = pltpu.VMEM((8, 128), F32)
        scratch[-3] = scratch[-2] = pltpu.SemaphoreType.DMA((1,))
    return pl.pallas_call(
        kernel,
        out_shape=(
            jax.ShapeDtypeStruct((nodes, width), BF16),
            pltpu.VMEM((nodes, width), BF16),
            pltpu.VMEM((clusters, CLUSTER, CLUSTER), BF16),
            pltpu.VMEM((R, width), F32)
            if linked
            else jax.ShapeDtypeStruct((Y, X, 2, SR, width), BF16),
            pltpu.VMEM((8, 128 if linked else width), F32),
        ),
        in_specs=[away] * 3 + [here, away],
        out_specs=(away, here, here, here if linked else away, here),
        scratch_shapes=scratch,
        compiler_params=pltpu.CompilerParams(
            collective_id=0 if linked else None,
            has_side_effects=True,
            vmem_limit_bytes=48 * 2**20,
        ),
        name="layer",
    )


def make_last(dp_size, shard_size, rows, width, nodes):
    clusters = nodes // CLUSTER
    per_cluster = width // PC
    steps = clusters * per_cluster
    part_rows = nodes // steps
    linked = linkable(rows)

    def kernel(links, spread, act_in, gw_in, gb_in, out, act_out, gw_out, gb_out, held, tiles, sem):
        def inward(k):
            part = act_in.at[pl.ds(pl.multiple_of(k * part_rows, part_rows), part_rows)]
            return pltpu.make_async_copy(part, held.at[k], sem.at[k])

        def outward(k):
            part = act_out.at[pl.ds(pl.multiple_of(k * part_rows, part_rows), part_rows)]
            return pltpu.make_async_copy(held.at[k], part, sem.at[steps + k])

        def place(k):
            return (
                pl.ds(pl.multiple_of(k // per_cluster * CLUSTER, CLUSTER), CLUSTER),
                pl.ds(pl.multiple_of(k % per_cluster * PC, PC), PC),
            )

        def store(k):
            return pltpu.make_async_copy(
                tiles.at[k % 2], out.at[place(k)], sem.at[2 * steps + k % 2]
            )

        carry = pltpu.make_async_copy(gw_in, gw_out, sem.at[2 * steps + 2])
        @pl.loop(0, steps)
        def _(k):
            inward(k).start()

        if linked:
            carry.start()
            me = Place(dp_size, shard_size)
            total = jnp.sum(gb_in[...], axis=0, keepdims=True)
            total = jnp.broadcast_to(total, (8, 128))
            gb_out[...] = pltpu.roll(total, (128 - me.lane(rows)) % 128, 1)[0:1, :rows]

        @pl.loop(0, steps)
        def _(k):
            pl.when(k >= 2)(lambda: store(k - 2).wait())
            tiles[k % 2] = dot(links[k // per_cluster], spread[place(k)], NN)
            store(k).start()
            inward(k).wait()
            outward(k).start()

        @pl.loop(0, steps)
        def _(k):
            outward(k).wait()

        for k in (steps - 2, steps - 1):
            store(k).wait()
        if linked:
            carry.wait()

    away = pl.BlockSpec(memory_space=pltpu.HBM)
    here = pl.BlockSpec(memory_space=pltpu.VMEM)
    return pl.pallas_call(
        kernel,
        out_shape=(
            jax.ShapeDtypeStruct((nodes, width), F32),
            jax.ShapeDtypeStruct((nodes, width), BF16),
            jax.ShapeDtypeStruct((rows, width), F32),
            jax.ShapeDtypeStruct((1, rows), F32),
        ),
        in_specs=[here, here, away, here, here],
        out_specs=(away, away, away, here),
        scratch_shapes=[
            pltpu.VMEM((steps, part_rows, width), BF16),
            pltpu.VMEM((2, CLUSTER, PC), F32),
            pltpu.SemaphoreType.DMA((2 * steps + 3,)),
        ],
        compiler_params=pltpu.CompilerParams(vmem_limit_bytes=14 * 2**20),
        name="features",
    )


def solution(mesh):
    dp_size, shard_size = mesh.shape["dp"], mesh.shape["shard"]

    def keep(array):
        return pltpu.with_memory_space_constraint(array, pltpu.VMEM)

    def leave(array):
        return pltpu.with_memory_space_constraint(array, pltpu.HBM)

    def on_device(features, neighbors, weight, bias_terms, grad_out):
        nodes, width = features.shape
        rows = weight.shape[0]
        layer = make_kernel(dp_size, shard_size, rows, width, nodes)
        last = make_last(dp_size, shard_size, rows, width, nodes)
        if linkable(rows):
            act, spread, links, grad_weight, bias_sums = layer(
                features, neighbors, weight, bias_terms.reshape(1, rows), grad_out
            )
            grad_features, output, grad_weight, grad_bias = last(
                keep(links), keep(spread), leave(act), keep(grad_weight), keep(bias_sums)
            )
            return output, grad_features, grad_weight, grad_bias.reshape(rows)
        both = ("dp", "shard")
        full = lax.all_gather(weight, both, axis=0, tiled=True)
        bias = lax.all_gather(bias_terms, both, axis=0, tiled=True).astype(F32)
        act, spread, links, parts, bias_sums = layer(
            features,
            neighbors,
            full.reshape(dp_size // 4, 2, 2, shard_size * rows, width),
            jnp.broadcast_to(bias, (8, width)),
            grad_out,
        )
        grad_features, output, *_ = last(
            keep(links),
            keep(spread),
            leave(act),
            jnp.zeros((rows, width), F32),
            jnp.zeros((8, 128), F32),
        )
        parts = parts.reshape(width, width).astype(F32)
        bias_sums = jnp.sum(bias_sums, axis=0)
        return (
            output,
            grad_features,
            lax.psum_scatter(parts, both, scatter_dimension=0, tiled=True),
            lax.psum_scatter(bias_sums, both, scatter_dimension=0, tiled=True),
        )

    split = P(("dp", "shard"), None)
    flat = P(("dp", "shard"))
    return jax.shard_map(
        on_device,
        mesh=mesh,
        in_specs=(split, split, split, flat, split),
        out_specs=(split, split, split, flat),
        check_vma=False,
    )
```

```python
import jax
import jax.numpy as jnp
from jax import lax
from jax.experimental import pallas as pl
from jax.experimental.pallas import tpu as pltpu
from jax.sharding import PartitionSpec as P

F32, BF16, I32 = jnp.float32, jnp.bfloat16, jnp.int32
MESH = pl.DeviceIdType.MESH
CLUSTER = 1024
SLOTS = 128
UNROLL = 64
LOW = 32
PC = 512
HC = 256
GC = 256
ALPHA = 0.7978845608028654
BETA = ALPHA * 0.044715
NN = (((1,), (0,)), ((), ()))
TN = (((0,), (0,)), ((), ()))
NT = (((1,), (1,)), ((), ()))
ALL = slice(None)

GATHER = ("zxy", "zyx", "zxy", "zyx", "zxy", "zyx", "xzy", "yzx")
SCATTER = ("yzx", "xzy", "yxz", "xyz", "yxz", "xyz", "yxz", "xyz")
COUNT_EVENTS = (
    (4, "second", 0),
    (6, "first", 2),
    (8, "third", 0),
    (8, "second", 1),
    (12, "second", 3),
    (12, "second", 2),
)
MIX_EVENTS = (
    (0, "third", 1),
    (0, "pass", 0),
    (3, "third", 2),
    (7, "third", 3),
    (7, "pass", 1),
)
PANEL_GATHER = (
    (0, "ready", 1),
    (3, "pass", 2),
    (4, "ready", 2),
    (6, "pass", 3),
    (8, "ready", 3),
)
PANEL_SCATTER = ((9, 1, 0), (13, 1, 1), (15, 2, 0), (17, 2, 1))
BACK_SCATTER = (
    (0, 3, 0),
    (0, 1, 2),
    (2, 3, 1),
    (3, 2, 2),
    (4, 1, 3),
    (6, 3, 2),
    (6, 2, 3),
)


def dot(a, b, dims):
    return lax.dot_general(a, b, dims, preferred_element_type=F32)


class Place:
    def __init__(self, dp_size, shard_size):
        dp, self.z = lax.axis_index("dp"), lax.axis_index("shard")
        self.dp = dp
        self.c, self.x, self.y = dp % 2, (dp // 2) % 2, dp // 4
        self.size = {"c": 2, "x": 2, "y": dp_size // 4, "z": shard_size}

    def at(self, dim):
        return {"c": self.c, "x": self.x, "y": self.y, "z": self.z}[dim]

    def shifted(self, dim, offset):
        size = self.size[dim]
        return lax.rem(self.at(dim) + (offset + size), size)

    def peer(self, dim, offset):
        other = self.shifted(dim, offset)
        if dim == "z":
            return (self.dp, other)
        step = {"c": 1, "x": 2, "y": 4}[dim]
        return (self.dp + step * (other - self.at(dim)), self.z)

    def lane(self, rows):
        return (self.dp * self.size["z"] + self.z) * rows % 128

    def offsets(self, dim):
        return range(1, self.size[dim])


class Sems:
    def __init__(self):
        self.index = {}

    def __getitem__(self, name):
        return self.index.setdefault(name, len(self.index))


def sem_names(sizes):
    sems = Sems()
    for t in list(range(len(GATHER))) + ["bias"]:
        path = GATHER[0] if t == "bias" else GATHER[t]
        for k in range(3):
            for o in range(1, sizes[path[k]]):
                sems["gather", t, k, o]
        sems["core", t, 0]
        for o in range(1, sizes[path[2]]):
            sems["core", t, o]
    for t in list(range(len(SCATTER))) + ["bias"]:
        path = SCATTER[0] if t == "bias" else SCATTER[t]
        for k in range(3):
            for o in range(1, sizes[path[k]]):
                sems["scatter", t, k, o]
    sems["swap", "bias"]
    for j in range(len(SCATTER) // 2):
        sems["swap", j]
    return sems


def linkable(rows):
    return rows % 16 == 0


def make_kernel(dp_size, shard_size, rows, width, nodes):
    sizes = {"c": 2, "x": 2, "y": dp_size // 4, "z": shard_size}
    Y, X, S, R = sizes["y"], 2, shard_size, rows
    SR = S * R
    n_dev = dp_size * shard_size
    panels = width // PC
    half_rows = width // 2
    clusters = nodes // CLUSTER
    sems = sem_names(sizes)
    n_sems = len(sems.index)
    chunks = nodes // 128
    TM = 512
    tiles = (nodes // TM) * panels
    per_panel = nodes // TM
    BM = 256

    def stage_shape(path, k):
        n = sizes[path[k]] - 1
        left = path[k + 1 :]
        lead = tuple(sizes[d] for d in "yx" if d in left)
        return (n,) + lead, ("z" in left)

    def stage_shapes():
        out = []
        for t in range(len(SCATTER)):
            for k in range(3):
                lead, z = stage_shape(SCATTER[t], k)
                out.append(pltpu.VMEM(lead + (SR if z else R, HC), BF16))
        for k in range(3):
            lead, z = stage_shape(SCATTER[0], k)
            out.append(pltpu.VMEM(lead + (S if z else 1, 8, 128), F32))
        return out

    n_stage = 3 * (len(SCATTER) + 1)
    linked = linkable(rows)

    def kernel(
        f_hbm, n_hbm, w_hbm, b_in, g_hbm,
        act_hbm, fg, a2t, gw_out, gb_out,
        mixed, wg, fac, b_own, bt, brow, gbacc, cr, crb, ptb, *rest,
    ):
        stage = rest[:n_stage]
        ssem, rsem, lsem = rest[n_stage:]
        me = Place(dp_size, shard_size)
        c, x, y, z = me.c, me.x, me.y, me.z
        started = {}

        def remote(name, src, dst, device):
            i = sems[name]
            return pltpu.make_async_remote_copy(
                src_ref=src, dst_ref=dst, send_sem=ssem.at[i], recv_sem=rsem.at[i],
                device_id=device, device_id_type=MESH,
            )

        def send(name, make):
            remote(name, *make()).start()
            started[name] = make

        def arrived(name, ref):
            remote(name, ref, ref, me.peer("c", 1)).wait_recv()

        def view(t, core, **at):
            ys, xs = at.get("y", ALL), at.get("x", ALL)
            if t == "bias":
                zs = pl.ds(at["z"], 1) if "z" in at else ALL
                return bt.at[ys, xs, core, zs]
            zs = pl.ds(pl.multiple_of(at["z"] * R, R), R) if "z" in at else ALL
            return wg.at[t // 2, ys, xs, core, zs, pl.ds(t % 2 * HC, HC)]

        own = {"x": x, "y": y, "z": z}

        def fixed(dims):
            return {d: own[d] for d in dims}

        def gather_path(t):
            return GATHER[0] if t == "bias" else GATHER[t]

        def gather_first(t):
            path = gather_path(t)

            def make(o):
                if t == "bias":
                    return b_own, bt.at[y, x, c, z], me.peer(path[0], o)
                src = w_hbm.at[:, pl.ds(t * HC, HC)]
                return src, view(t, c, **fixed("xyz")), me.peer(path[0], o)

            for o in me.offsets(path[0]):
                send(("gather", t, 0, o), lambda o=o: make(o))

        def gather_wait(t, k):
            path = gather_path(t)
            for o in me.offsets(path[k]):
                at = fixed(path[k:])
                at[path[k]] = me.shifted(path[k], -o)
                arrived(("gather", t, k, o), view(t, c, **at))

        def gather_send(t, k):
            path = gather_path(t)

            def make(o):
                ref = view(t, c, **fixed(path[k:]))
                return ref, ref, me.peer(path[k], o)

            for o in me.offsets(path[k]):
                send(("gather", t, k, o), lambda o=o: make(o))

        def core_send(t, late):
            path = gather_path(t)

            def make(o):
                at = {path[2]: me.shifted(path[2], -o)} if o else fixed(path[2:])
                ref = view(t, c, **at)
                return ref, ref, me.peer("c", 1)

            for o in me.offsets(path[2]) if late else (0,):
                send(("core", t, o), lambda o=o: make(o))

        def core_wait(t):
            path = gather_path(t)
            arrived(("core", t, 0), view(t, 1 - c, **fixed(path[2:])))
            for o in me.offsets(path[2]):
                arrived(
                    ("core", t, o),
                    view(t, 1 - c, **{path[2]: me.shifted(path[2], -o)}),
                )

        def slices(panel):
            return (2 * panel, 2 * panel + 1) + (("bias",) if panel == 0 else ())

        def own_block(j):
            if not linked:
                return pltpu.make_async_copy(
                    w_hbm.at[:, :, :, :, pl.ds(j * PC, PC)], wg.at[j], lsem.at[8 + j]
                )
            return pltpu.make_async_copy(
                w_hbm.at[:, pl.ds(j * PC, PC)],
                wg.at[j, y, x, c, pl.ds(pl.multiple_of(z * R, R), R), :],
                lsem.at[8 + j],
            )

        def own_bias():
            return pltpu.make_async_copy(b_own, bt.at[y, x, c, z], lsem.at[8 + panels])

        def gather_event(kind, panel):
            if not linked:
                if kind == "ready":
                    own_block(panel).wait()
            elif kind == "first":
                for t in slices(panel):
                    gather_first(t)
            elif kind == "second":
                for t in slices(panel):
                    gather_wait(t, 0)
                own_block(panel).wait()
                if panel == 0:
                    own_bias().wait()
                for t in slices(panel):
                    gather_send(t, 1)
            elif kind == "third":
                for t in slices(panel):
                    gather_wait(t, 1)
                for t in slices(panel):
                    gather_send(t, 2)
                for t in slices(panel):
                    core_send(t, False)
            elif kind == "pass":
                for t in slices(panel):
                    gather_wait(t, 2)
                for t in slices(panel):
                    core_send(t, True)
            elif kind == "ready":
                for t in slices(panel):
                    core_wait(t)

        load_n = lambda ref: pltpu.make_async_copy(n_hbm, ref, lsem.at[9 + panels])
        load_f = pltpu.make_async_copy(f_hbm, fg, lsem.at[10 + panels])

        def count_phase(nb, low, *digits):
            load_n(nb).start()
            peers = [me.peer(d, o) for d in "cxyz" for o in me.offsets(d) if linked]
            for p in peers:
                pl.semaphore_signal(
                    pltpu.get_barrier_semaphore(), inc=1,
                    device_id=p, device_id_type=MESH,
                )
            for j in range(panels):
                own_block(j).start()
            if linked:
                bias = b_in[...].astype(F32)
                bias = jnp.concatenate([bias, jnp.zeros((1, 128 - R), F32)], axis=1)
                bias = jnp.broadcast_to(bias, (8, 128))
                b_own[...] = pltpu.roll(bias, me.lane(R), 1)
                own_bias().start()
                pl.semaphore_wait(pltpu.get_barrier_semaphore(), len(peers))
            gather_event("first", 0)
            gather_event("first", 3)
            load_f.start()
            load_n(nb).wait()

            @pl.loop(0, chunks)
            def _(q):
                r = pl.ds(pl.multiple_of(q * 128, 128), 128)
                ids = nb[r, :]
                degree = jnp.sum((ids >= 0).astype(F32), axis=1, keepdims=True)
                fac[r, :] = jnp.broadcast_to(1.0 / (degree + 1.0), (128, 128))
                ids = ids.T
                high = ids >> (LOW.bit_length() - 1)
                digit = jnp.left_shift(jnp.ones_like(ids), (high & 3) * 8)
                low[:, r] = ids & (LOW - 1)
                for k, ref in enumerate(digits):
                    ref[:, r] = jnp.where(high >> 2 == k, digit, 0)

            gather_event("first", 1)
            place_in = lax.broadcasted_iota(I32, (LOW, 128), 0)
            lane = lax.broadcasted_iota(I32, (LOW, 128), 1)

            @pl.loop(0, chunks)
            def _(q):
                col = pl.ds(pl.multiple_of(q * 128, 128), 128)

                def step(s, carry):
                    some = pl.ds(pl.multiple_of(s * UNROLL, UNROLL), UNROLL)
                    lo, add = low[some, col], [ref[some, col] for ref in digits]
                    for k in range(UNROLL):
                        hit = lo[k : k + 1] == place_in
                        carry = tuple(
                            total + jnp.where(hit, a[k : k + 1], 0)
                            for total, a in zip(carry, add)
                        )
                    return carry

                zero = (jnp.zeros((LOW, 128), I32),) * len(digits)
                totals = lax.fori_loop(0, SLOTS // UNROLL, step, zero)
                cl, place = q // 8, q % 8
                to = pl.ds(pl.multiple_of(place * 128, 128), 128)
                for b in range(CLUSTER // LOW):
                    count = ((totals[b // 4] >> (8 * (b % 4))) & 255).astype(F32)
                    self_at = place * 128 - b * LOW
                    count = count + jnp.where(place_in - lane == self_at, 2.0, 0.0)
                    a2t[cl, pl.ds(b * LOW, LOW), to] = count.astype(BF16)
                for at, kind, panel in COUNT_EVENTS:
                    pl.when(q == at)(lambda k=kind, p=panel: gather_event(k, p))

        pl.run_scoped(
            count_phase,
            pltpu.VMEM((nodes, SLOTS), I32),
            *[pltpu.VMEM((SLOTS, nodes), I32)] * (1 + CLUSTER // LOW // 4),
        )
        load_f.wait()

        @pl.loop(0, clusters * 4)
        def _(s):
            cl, i, j = s // 4, (s // 2) % 2, s % 2
            r = pl.ds(pl.multiple_of(cl * CLUSTER + i * 512, 512), 512)
            k = pl.ds(pl.multiple_of(cl * CLUSTER, CLUSTER), CLUSTER)
            col = pl.ds(pl.multiple_of(j * half_rows, half_rows), half_rows)
            links = a2t[cl, :, pl.ds(pl.multiple_of(i * 512, 512), 512)]
            total = dot(links, fg[k, col], TN)
            scale = jnp.concatenate([fac[r, :]] * (half_rows // 128), axis=1)
            mixed[r, col] = (scale * total).astype(BF16)
            for at, kind, panel in MIX_EVENTS:
                pl.when(s == at)(lambda k=kind, p=panel: gather_event(k, p))

        def part(pt, t, **at):
            ys, xs = at.get("y", ALL), at.get("x", ALL)
            if t == "bias":
                zs = pl.ds(at["z"], 1) if "z" in at else ALL
                return ptb.at[ys, xs, c, zs]
            zs = pl.ds(pl.multiple_of(at["z"] * R, R), R) if "z" in at else ALL
            return pt.at[t // 2, ys, xs, zs, pl.ds(t % 2 * HC, HC)]

        def scatter_path(t):
            return SCATTER[0] if t == "bias" else SCATTER[t]

        def landing(t, k):
            return stage[(len(SCATTER) if t == "bias" else t) * 3 + k]

        def scatter_send(pt, t, k):
            path = scatter_path(t)

            def make(o):
                at = fixed(path[:k])
                at[path[k]] = me.shifted(path[k], o)
                return part(pt, t, **at), landing(t, k).at[o - 1], me.peer(path[k], o)

            for o in me.offsets(path[k]):
                send(("scatter", t, k, o), lambda o=o: make(o))

        def scatter_wait(t, k):
            for o in me.offsets(scatter_path(t)[k]):
                arrived(("scatter", t, k, o), landing(t, k).at[o - 1])

        def over_rows(shape, action):
            lead, high = shape[:-2], shape[-2]
            step = min(high, 64)

            def walk(index):
                if len(index) < len(lead):
                    if lead[len(index)] == 1:
                        walk(index + (0,))
                    else:
                        pl.loop(0, lead[len(index)])(lambda k: walk(index + (k,)))
                elif high == step:
                    action(index + (pl.ds(0, step),))
                else:
                    pl.loop(0, high // step)(
                        lambda k: action(
                            index + (pl.ds(pl.multiple_of(k * step, step), step),)
                        )
                    )

            walk(())

        def scatter_add(pt, t, k):
            path = scatter_path(t)
            mine = part(pt, t, **fixed(path[: k + 1]))
            others = [landing(t, k).at[o - 1] for o in me.offsets(path[k])]
            if t == "bias":
                total = mine[...]
                for other in others:
                    total = total + other[...]
                if k < 2:
                    mine[...] = total
                else:
                    gb_out[...] = total.reshape(8, 128)
                return

            def piece(at):
                total = mine[at].astype(F32)
                for other in others:
                    total = total + other[at].astype(F32)
                if k < 2:
                    mine[at] = total.astype(BF16)
                else:
                    gw_out[at[0], pl.ds(t * HC, HC)] = total

            over_rows(mine.shape, piece)

        def swap(po, j):
            i = sems["swap", 0] + j
            return pltpu.make_async_remote_copy(
                src_ref=po.at[j], dst_ref=cr.at[j],
                send_sem=ssem.at[i], recv_sem=rsem.at[i],
                device_id=me.peer("c", 1), device_id_type=MESH,
            )

        def scatter_event(pt, k, j):
            ts = (2 * j, 2 * j + 1) + (("bias",) if j == panels - 1 else ())
            for t in ts:
                scatter_wait(t, k - 1)
                scatter_add(pt, t, k - 1)
                if k < 3:
                    scatter_send(pt, t, k)

        def store_part(held, j, core, k):
            col = pl.ds(pl.multiple_of(j * PC, PC), PC)
            return pltpu.make_async_copy(
                held.at[j],
                gw_out.at[:, :, core, :, col],
                lsem.at[12 + (1 + k) * panels + j],
            )

        def panel_phase(pt, po, acc_a, acc_b, go, ac):
            def tile_rows(i):
                return pl.ds(pl.multiple_of(i * TM, TM), TM)

            def block(hbm, j, i):
                return hbm.at[tile_rows(i), pl.ds(pl.multiple_of(j * PC, PC), PC)]

            def load_g(j, i):
                return pltpu.make_async_copy(block(g_hbm, j, i), go.at[i], lsem.at[i])

            def store_act(j, i):
                return pltpu.make_async_copy(
                    ac.at[i], block(act_hbm, j, i), lsem.at[4 + i]
                )

            def product(j, i, cols):
                panel = wg[j, :, :, :, :, cols].reshape(width, GC)
                return dot(mixed[tile_rows(i), :], panel, NN)

            def finish(acc, j, i, cols):
                r = tile_rows(i)
                col = pl.ds(pl.multiple_of(j * PC + cols.start, GC), GC)
                v = acc[:, cols] + brow[0:1, col]
                u = v * v
                h = 0.5 + 0.5 * jnp.tanh(v * (ALPHA + BETA * u))
                a = v * h
                d = h + (a * (1.0 - h)) * (2 * ALPHA + (6 * BETA) * u)
                g = go[i, :, cols].astype(F32) * d
                ac[i, :, cols] = a.astype(BF16)
                fg[r, col] = g.astype(BF16)
                gbacc[:, col] += jnp.sum(g.reshape(TM // 8, 8, GC), axis=0)

            def weight_rows(j, core):
                lhs = [
                    mixed[:, pl.ds(pl.multiple_of((b * 2 + core) * SR, SR), SR)]
                    for b in range(Y * X)
                ]
                col = pl.ds(pl.multiple_of(j * PC, PC), PC)
                total = dot(jnp.concatenate(lhs, axis=1), fg[:, col], TN)
                return total.reshape(Y, X, SR, PC)

            def events(step):
                for at, kind, panel in PANEL_GATHER:
                    pl.when(step == at)(lambda k=kind, p=panel: gather_event(k, p))
                if not linked:
                    return
                for at, k, panel in PANEL_SCATTER:
                    pl.when(step == at)(lambda k=k, p=panel: scatter_event(pt, k, p))

            def send_bias():
                for d in range(n_dev):
                    col = pl.ds(d * R // 128 * 128, 128)
                    at = (d // (X * 2 * S), d // (2 * S) % X, d // S % 2, d % S)
                    ptb[at] = gbacc[:, col]
                send(
                    ("swap", "bias"),
                    lambda: (ptb.at[:, :, 1 - c], crb, me.peer("c", 1)),
                )

            def sum_bias():
                arrived(("swap", "bias"), crb)
                mine = ptb.at[:, :, c]
                mine[...] = mine[...] + crb[...]
                scatter_send(pt, "bias", 0)

            def pair(j, h):
                for k in range(2):
                    load_g(j, 2 * h + k).wait()
                    pl.when(j > 0)(lambda i=2 * h + k: store_act(j - 1, i).wait())
                for k, acc, other in ((0, acc_a, acc_b), (1, acc_b, acc_a)):
                    i = 2 * h + k
                    n = jnp.minimum(j * per_panel + i + 1, tiles - 1)
                    for q in range(PC // GC):
                        cols = pl.ds(q * GC, GC)
                        other[:, cols] = product(n // per_panel, n % per_panel, cols)
                        finish(acc, j, i, cols)
                for k in range(2):
                    i = 2 * h + k
                    store_act(j, i).start()
                    pl.when(j < panels - 1)(lambda i=i: load_g(j + 1, i).start())

            def own_rows(j):
                total = weight_rows(j, c)
                if linked:
                    swap(po, j).wait_recv()
                    total = total + cr[j].astype(F32)
                pt[j] = total.astype(BF16)
                if not linked:
                    store_part(pt, j, c, 0).start()
                    return
                for p in range(panels):

                    @pl.when(j == p)
                    def _():
                        for t in (2 * p, 2 * p + 1):
                            scatter_send(pt, t, 0)
                        if p == panels - 1:
                            sum_bias()

            def other_rows(j):
                po[j] = weight_rows(j, 1 - c).astype(BF16)
                if linked:
                    swap(po, j).start()
                    pl.when(j == panels - 1)(send_bias)
                else:
                    store_part(po, j, 1 - c, 1).start()

            def panel(j):
                @pl.loop(0, 2)
                def _(h):
                    pl.when(j < panels)(lambda: pair(j, h))
                    events(4 * j + 2 * h)
                    pl.when((h == 0) & (j > 0))(lambda: own_rows(j - 1))
                    pl.when((h == 1) & (j < panels))(lambda: other_rows(j))
                    events(4 * j + 2 * h + 1)

            for i in range(per_panel):
                load_g(0, i).start()
            gather_event("ready", 0)
            p = 128 // R
            if not linked:
                brow[...] = b_in[...]
            for k in range(width // 128 if linked else 0):
                tile = jnp.zeros((8, 128), F32)
                for d in range(k * p, (k + 1) * p):
                    tile = tile + bt[d // (X * 2 * S), d // (2 * S) % X, d // S % 2, d % S]
                brow[:, pl.ds(k * 128, 128)] = tile
            gbacc[...] = jnp.zeros_like(gbacc)
            for q in range(PC // GC):
                cols = pl.ds(q * GC, GC)
                acc_a[:, cols] = product(0, 0, cols)
            pl.loop(0, panels + 1)(panel)
            for i in range(per_panel):
                store_act(panels - 1, i).wait()

        def back_phase(pt, po):
            steps = nodes // BM

            @pl.loop(0, steps)
            def _(s):
                r = pl.ds(pl.multiple_of(s * BM, BM), BM)
                total = None
                for j in range(panels):
                    rhs = wg[j].reshape(width, PC)
                    term = dot(fg[r, pl.ds(j * PC, PC)], rhs, NT)
                    total = term if total is None else total + term
                scale = jnp.concatenate([fac[r, :]] * (width // 128), axis=1)
                fg[r, :] = (scale * total).astype(BF16)
                if not linked:
                    return

                for at, k, panel in BACK_SCATTER:
                    pl.when(s == at)(lambda k=k, p=panel: scatter_event(pt, k, p))

            if linked:
                scatter_event(pt, 3, panels - 1)
                for j in range(panels):
                    swap(po, j).wait_send()
                for name, make in started.items():
                    remote(name, *make()).wait_send()
            else:
                for j in range(panels):
                    store_part(pt, j, c, 0).wait()
                    store_part(po, j, 1 - c, 1).wait()
                gb_out[...] = gbacc[...]

        def with_parts(pt, po):
            pl.run_scoped(
                lambda *refs: panel_phase(pt, po, *refs),
                *[pltpu.VMEM((TM, PC), F32)] * 2,
                *[pltpu.VMEM((per_panel, TM, PC), BF16)] * 2,
            )
            back_phase(pt, po)

        pl.run_scoped(with_parts, *[pltpu.VMEM((panels, Y, X, SR, PC), BF16)] * 2)

    away = pl.BlockSpec(memory_space=pltpu.HBM)
    here = pl.BlockSpec(memory_space=pltpu.VMEM)
    scratch = [
        pltpu.VMEM((nodes, width), BF16),
        pltpu.VMEM((panels, Y, X, 2, SR, PC), BF16),
        pltpu.VMEM((nodes, 128), F32),
        pltpu.VMEM((8, 128), F32),
        pltpu.VMEM((Y, X, 2, S, 8, 128), F32),
        pltpu.VMEM((8, width), F32),
        pltpu.VMEM((8, width), F32),
        pltpu.VMEM((panels, Y, X, SR, PC), BF16),
        pltpu.VMEM((Y, X, S, 8, 128), F32),
        pltpu.VMEM((Y, X, 2, S, 8, 128), F32),
        *stage_shapes(),
        pltpu.SemaphoreType.DMA((n_sems,)),
        pltpu.SemaphoreType.DMA((n_sems,)),
        pltpu.SemaphoreType.DMA((12 + 3 * panels,)),
    ]
    if not linked:
        for k in (3, 4, 7, 8, 9, *range(10, 10 + n_stage)):
            scratch[k] = pltpu.VMEM((8, 128), F32)
        scratch[-3] = scratch[-2] = pltpu.SemaphoreType.DMA((1,))
    return pl.pallas_call(
        kernel,
        out_shape=(
            jax.ShapeDtypeStruct((nodes, width), BF16),
            pltpu.VMEM((nodes, width), BF16),
            pltpu.VMEM((clusters, CLUSTER, CLUSTER), BF16),
            pltpu.VMEM((R, width), F32)
            if linked
            else jax.ShapeDtypeStruct((Y, X, 2, SR, width), BF16),
            pltpu.VMEM((8, 128 if linked else width), F32),
        ),
        in_specs=[away] * 3 + [here, away],
        out_specs=(away, here, here, here if linked else away, here),
        scratch_shapes=scratch,
        compiler_params=pltpu.CompilerParams(
            collective_id=0 if linked else None,
            has_side_effects=True,
            vmem_limit_bytes=48 * 2**20,
        ),
        name="layer",
    )


def make_last(dp_size, shard_size, rows, width, nodes):
    clusters = nodes // CLUSTER
    per_cluster = width // PC
    steps = clusters * per_cluster
    part_rows = nodes // steps
    linked = linkable(rows)

    def kernel(links, spread, act_in, gw_in, gb_in, out, act_out, gw_out, gb_out, held, tiles, sem):
        def inward(k):
            part = act_in.at[pl.ds(pl.multiple_of(k * part_rows, part_rows), part_rows)]
            return pltpu.make_async_copy(part, held.at[k], sem.at[k])

        def outward(k):
            part = act_out.at[pl.ds(pl.multiple_of(k * part_rows, part_rows), part_rows)]
            return pltpu.make_async_copy(held.at[k], part, sem.at[steps + k])

        def place(k):
            return (
                pl.ds(pl.multiple_of(k // per_cluster * CLUSTER, CLUSTER), CLUSTER),
                pl.ds(pl.multiple_of(k % per_cluster * PC, PC), PC),
            )

        def store(k):
            return pltpu.make_async_copy(
                tiles.at[k % 2], out.at[place(k)], sem.at[2 * steps + k % 2]
            )

        carry = pltpu.make_async_copy(gw_in, gw_out, sem.at[2 * steps + 2])
        @pl.loop(0, steps)
        def _(k):
            inward(k).start()

        if linked:
            carry.start()
            me = Place(dp_size, shard_size)
            total = jnp.sum(gb_in[...], axis=0, keepdims=True)
            total = jnp.broadcast_to(total, (8, 128))
            gb_out[...] = pltpu.roll(total, (128 - me.lane(rows)) % 128, 1)[0:1, :rows]

        @pl.loop(0, steps)
        def _(k):
            pl.when(k >= 2)(lambda: store(k - 2).wait())
            tiles[k % 2] = dot(links[k // per_cluster], spread[place(k)], NN)
            store(k).start()
            inward(k).wait()
            outward(k).start()

        @pl.loop(0, steps)
        def _(k):
            outward(k).wait()

        for k in (steps - 2, steps - 1):
            store(k).wait()
        if linked:
            carry.wait()

    away = pl.BlockSpec(memory_space=pltpu.HBM)
    here = pl.BlockSpec(memory_space=pltpu.VMEM)
    return pl.pallas_call(
        kernel,
        out_shape=(
            jax.ShapeDtypeStruct((nodes, width), F32),
            jax.ShapeDtypeStruct((nodes, width), BF16),
            jax.ShapeDtypeStruct((rows, width), F32),
            jax.ShapeDtypeStruct((1, rows), F32),
        ),
        in_specs=[here, here, away, here, here],
        out_specs=(away, away, away, here),
        scratch_shapes=[
            pltpu.VMEM((steps, part_rows, width), BF16),
            pltpu.VMEM((2, CLUSTER, PC), F32),
            pltpu.SemaphoreType.DMA((2 * steps + 3,)),
        ],
        compiler_params=pltpu.CompilerParams(vmem_limit_bytes=14 * 2**20),
        name="features",
    )


def solution(mesh):
    dp_size, shard_size = mesh.shape["dp"], mesh.shape["shard"]

    def keep(array):
        return pltpu.with_memory_space_constraint(array, pltpu.VMEM)

    def leave(array):
        return pltpu.with_memory_space_constraint(array, pltpu.HBM)

    def on_device(features, neighbors, weight, bias_terms, grad_out):
        nodes, width = features.shape
        rows = weight.shape[0]
        layer = make_kernel(dp_size, shard_size, rows, width, nodes)
        last = make_last(dp_size, shard_size, rows, width, nodes)
        if linkable(rows):
            act, spread, links, grad_weight, bias_sums = layer(
                features, neighbors, weight, bias_terms.reshape(1, rows), grad_out
            )
            grad_features, output, grad_weight, grad_bias = last(
                keep(links), keep(spread), leave(act), keep(grad_weight), keep(bias_sums)
            )
            return output, grad_features, grad_weight, grad_bias.reshape(rows)
        both = ("dp", "shard")
        full = lax.all_gather(weight, both, axis=0, tiled=True)
        bias = lax.all_gather(bias_terms, both, axis=0, tiled=True).astype(F32)
        act, spread, links, parts, bias_sums = layer(
            features,
            neighbors,
            full.reshape(dp_size // 4, 2, 2, shard_size * rows, width),
            jnp.broadcast_to(bias, (8, width)),
            grad_out,
        )
        grad_features, output, *_ = last(
            keep(links),
            keep(spread),
            leave(act),
            jnp.zeros((rows, width), F32),
            jnp.zeros((8, 128), F32),
        )
        parts = parts.reshape(width, width).astype(F32)
        bias_sums = jnp.sum(bias_sums, axis=0)
        return (
            output,
            grad_features,
            lax.psum_scatter(parts, both, scatter_dimension=0, tiled=True),
            lax.psum_scatter(bias_sums, both, scatter_dimension=0, tiled=True),
        )

    split = P(("dp", "shard"), None)
    flat = P(("dp", "shard"))
    return jax.shard_map(
        on_device,
        mesh=mesh,
        in_specs=(split, split, split, flat, split),
        out_specs=(split, split, split, flat),
        check_vma=False,
    )
```

```python
import jax
import jax.numpy as jnp
from jax import lax
from jax.experimental import pallas as pl
from jax.experimental.pallas import tpu as pltpu
from jax.sharding import PartitionSpec as P

F32, BF16, I32 = jnp.float32, jnp.bfloat16, jnp.int32
MESH = pl.DeviceIdType.MESH
CLUSTER = 1024
SLOTS = 128
UNROLL = 64
LOW = 32
PC = 512
HC = 256
GC = 256
ALPHA = 0.7978845608028654
BETA = ALPHA * 0.044715
NN = (((1,), (0,)), ((), ()))
TN = (((0,), (0,)), ((), ()))
NT = (((1,), (1,)), ((), ()))
ALL = slice(None)

GATHER = ("zxy", "zyx", "zxy", "zyx", "zxy", "zyx", "xzy", "yzx")
SCATTER = ("yzx", "xzy", "yxz", "xyz", "yxz", "xyz", "yxz", "xyz")
COUNT_EVENTS = (
    (4, "second", 0),
    (6, "first", 2),
    (8, "third", 0),
    (8, "second", 1),
    (12, "second", 3),
    (12, "second", 2),
)
MIX_EVENTS = (
    (0, "third", 1),
    (0, "pass", 0),
    (1, "third", 2),
    (3, "third", 3),
    (3, "pass", 1),
)
PANEL_GATHER = (
    (0, "ready", 1),
    (3, "pass", 2),
    (4, "ready", 2),
    (6, "pass", 3),
    (8, "ready", 3),
)
PANEL_SCATTER = ((9, 1, 0), (13, 1, 1), (15, 2, 0), (17, 2, 1))
BACK_SCATTER = (
    (0, 3, 0),
    (0, 1, 2),
    (2, 3, 1),
    (3, 2, 2),
    (4, 1, 3),
    (6, 3, 2),
    (6, 2, 3),
)


def dot(a, b, dims):
    return lax.dot_general(a, b, dims, preferred_element_type=F32)


class Place:
    def __init__(self, dp_size, shard_size):
        dp, self.z = lax.axis_index("dp"), lax.axis_index("shard")
        self.dp = dp
        self.c, self.x, self.y = dp % 2, (dp // 2) % 2, dp // 4
        self.size = {"c": 2, "x": 2, "y": dp_size // 4, "z": shard_size}

    def at(self, dim):
        return {"c": self.c, "x": self.x, "y": self.y, "z": self.z}[dim]

    def shifted(self, dim, offset):
        size = self.size[dim]
        return lax.rem(self.at(dim) + (offset + size), size)

    def peer(self, dim, offset):
        other = self.shifted(dim, offset)
        if dim == "z":
            return (self.dp, other)
        step = {"c": 1, "x": 2, "y": 4}[dim]
        return (self.dp + step * (other - self.at(dim)), self.z)

    def lane(self, rows):
        return (self.dp * self.size["z"] + self.z) * rows % 128

    def offsets(self, dim):
        return range(1, self.size[dim])


class Sems:
    def __init__(self):
        self.index = {}

    def __getitem__(self, name):
        return self.index.setdefault(name, len(self.index))


def sem_names(sizes):
    sems = Sems()
    for t in list(range(len(GATHER))) + ["bias"]:
        path = GATHER[0] if t == "bias" else GATHER[t]
        for k in range(3):
            for o in range(1, sizes[path[k]]):
                sems["gather", t, k, o]
        sems["core", t, 0]
        for o in range(1, sizes[path[2]]):
            sems["core", t, o]
    for t in list(range(len(SCATTER))) + ["bias"]:
        path = SCATTER[0] if t == "bias" else SCATTER[t]
        for k in range(3):
            for o in range(1, sizes[path[k]]):
                sems["scatter", t, k, o]
    sems["swap", "bias"]
    for j in range(len(SCATTER) // 2):
        sems["swap", j]
    return sems


def linkable(rows):
    return rows % 16 == 0


def make_kernel(dp_size, shard_size, rows, width, nodes):
    sizes = {"c": 2, "x": 2, "y": dp_size // 4, "z": shard_size}
    Y, X, S, R = sizes["y"], 2, shard_size, rows
    SR = S * R
    n_dev = dp_size * shard_size
    panels = width // PC
    half_rows = width // 2
    clusters = nodes // CLUSTER
    sems = sem_names(sizes)
    n_sems = len(sems.index)
    chunks = nodes // 128
    TM = 512
    tiles = (nodes // TM) * panels
    per_panel = nodes // TM
    BM = 256

    def stage_shape(path, k):
        n = sizes[path[k]] - 1
        left = path[k + 1 :]
        lead = tuple(sizes[d] for d in "yx" if d in left)
        return (n,) + lead, ("z" in left)

    def stage_shapes():
        out = []
        for t in range(len(SCATTER)):
            for k in range(3):
                lead, z = stage_shape(SCATTER[t], k)
                out.append(pltpu.VMEM(lead + (SR if z else R, HC), BF16))
        for k in range(3):
            lead, z = stage_shape(SCATTER[0], k)
            out.append(pltpu.VMEM(lead + (S if z else 1, 8, 128), F32))
        return out

    n_stage = 3 * (len(SCATTER) + 1)
    linked = linkable(rows)

    def kernel(
        f_hbm, n_hbm, w_hbm, b_in, g_hbm,
        act_hbm, fg, a2t, gw_out, gb_out,
        mixed, wg, fac, b_own, bt, brow, gbacc, cr, crb, ptb, *rest,
    ):
        stage = rest[:n_stage]
        ssem, rsem, lsem = rest[n_stage:]
        me = Place(dp_size, shard_size)
        c, x, y, z = me.c, me.x, me.y, me.z
        started = {}

        def remote(name, src, dst, device):
            i = sems[name]
            return pltpu.make_async_remote_copy(
                src_ref=src, dst_ref=dst, send_sem=ssem.at[i], recv_sem=rsem.at[i],
                device_id=device, device_id_type=MESH,
            )

        def send(name, make):
            remote(name, *make()).start()
            started[name] = make

        def arrived(name, ref):
            remote(name, ref, ref, me.peer("c", 1)).wait_recv()

        def view(t, core, **at):
            ys, xs = at.get("y", ALL), at.get("x", ALL)
            if t == "bias":
                zs = pl.ds(at["z"], 1) if "z" in at else ALL
                return bt.at[ys, xs, core, zs]
            zs = pl.ds(pl.multiple_of(at["z"] * R, R), R) if "z" in at else ALL
            return wg.at[t // 2, ys, xs, core, zs, pl.ds(t % 2 * HC, HC)]

        own = {"x": x, "y": y, "z": z}

        def fixed(dims):
            return {d: own[d] for d in dims}

        def gather_path(t):
            return GATHER[0] if t == "bias" else GATHER[t]

        def gather_first(t):
            path = gather_path(t)

            def make(o):
                if t == "bias":
                    return b_own, bt.at[y, x, c, z], me.peer(path[0], o)
                src = w_hbm.at[:, pl.ds(t * HC, HC)]
                return src, view(t, c, **fixed("xyz")), me.peer(path[0], o)

            for o in me.offsets(path[0]):
                send(("gather", t, 0, o), lambda o=o: make(o))

        def gather_wait(t, k):
            path = gather_path(t)
            for o in me.offsets(path[k]):
                at = fixed(path[k:])
                at[path[k]] = me.shifted(path[k], -o)
                arrived(("gather", t, k, o), view(t, c, **at))

        def gather_send(t, k):
            path = gather_path(t)

            def make(o):
                ref = view(t, c, **fixed(path[k:]))
                return ref, ref, me.peer(path[k], o)

            for o in me.offsets(path[k]):
                send(("gather", t, k, o), lambda o=o: make(o))

        def core_send(t, late):
            path = gather_path(t)

            def make(o):
                at = {path[2]: me.shifted(path[2], -o)} if o else fixed(path[2:])
                ref = view(t, c, **at)
                return ref, ref, me.peer("c", 1)

            for o in me.offsets(path[2]) if late else (0,):
                send(("core", t, o), lambda o=o: make(o))

        def core_wait(t):
            path = gather_path(t)
            arrived(("core", t, 0), view(t, 1 - c, **fixed(path[2:])))
            for o in me.offsets(path[2]):
                arrived(
                    ("core", t, o),
                    view(t, 1 - c, **{path[2]: me.shifted(path[2], -o)}),
                )

        def slices(panel):
            return (2 * panel, 2 * panel + 1) + (("bias",) if panel == 0 else ())

        def own_block(j):
            if not linked:
                return pltpu.make_async_copy(
                    w_hbm.at[:, :, :, :, pl.ds(j * PC, PC)], wg.at[j], lsem.at[8 + j]
                )
            return pltpu.make_async_copy(
                w_hbm.at[:, pl.ds(j * PC, PC)],
                wg.at[j, y, x, c, pl.ds(pl.multiple_of(z * R, R), R), :],
                lsem.at[8 + j],
            )

        def own_bias():
            return pltpu.make_async_copy(b_own, bt.at[y, x, c, z], lsem.at[8 + panels])

        def gather_event(kind, panel):
            if not linked:
                if kind == "ready":
                    own_block(panel).wait()
            elif kind == "first":
                for t in slices(panel):
                    gather_first(t)
            elif kind == "second":
                for t in slices(panel):
                    gather_wait(t, 0)
                own_block(panel).wait()
                if panel == 0:
                    own_bias().wait()
                for t in slices(panel):
                    gather_send(t, 1)
            elif kind == "third":
                for t in slices(panel):
                    gather_wait(t, 1)
                for t in slices(panel):
                    gather_send(t, 2)
                for t in slices(panel):
                    core_send(t, False)
            elif kind == "pass":
                for t in slices(panel):
                    gather_wait(t, 2)
                for t in slices(panel):
                    core_send(t, True)
            elif kind == "ready":
                for t in slices(panel):
                    core_wait(t)

        load_n = lambda ref: pltpu.make_async_copy(n_hbm, ref, lsem.at[9 + panels])
        load_f = pltpu.make_async_copy(f_hbm, fg, lsem.at[10 + panels])

        def count_phase(nb, low, *digits):
            load_n(nb).start()
            peers = [me.peer(d, o) for d in "cxyz" for o in me.offsets(d) if linked]
            for p in peers:
                pl.semaphore_signal(
                    pltpu.get_barrier_semaphore(), inc=1,
                    device_id=p, device_id_type=MESH,
                )
            for j in range(panels):
                own_block(j).start()
            if linked:
                bias = b_in[...].astype(F32)
                bias = jnp.concatenate([bias, jnp.zeros((1, 128 - R), F32)], axis=1)
                bias = jnp.broadcast_to(bias, (8, 128))
                b_own[...] = pltpu.roll(bias, me.lane(R), 1)
                own_bias().start()
                pl.semaphore_wait(pltpu.get_barrier_semaphore(), len(peers))
            gather_event("first", 0)
            gather_event("first", 3)
            load_f.start()
            load_n(nb).wait()

            @pl.loop(0, chunks)
            def _(q):
                r = pl.ds(pl.multiple_of(q * 128, 128), 128)
                ids = nb[r, :]
                degree = jnp.sum((ids >= 0).astype(F32), axis=1, keepdims=True)
                fac[r, :] = jnp.broadcast_to(1.0 / (degree + 1.0), (128, 128))
                ids = ids.T
                high = ids >> (LOW.bit_length() - 1)
                digit = jnp.left_shift(jnp.ones_like(ids), (high & 3) * 8)
                low[:, r] = ids & (LOW - 1)
                for k, ref in enumerate(digits):
                    ref[:, r] = jnp.where(high >> 2 == k, digit, 0)

            gather_event("first", 1)
            place_in = lax.broadcasted_iota(I32, (LOW, 128), 0)
            lane = lax.broadcasted_iota(I32, (LOW, 128), 1)

            @pl.loop(0, chunks)
            def _(q):
                col = pl.ds(pl.multiple_of(q * 128, 128), 128)

                def step(s, carry):
                    some = pl.ds(pl.multiple_of(s * UNROLL, UNROLL), UNROLL)
                    lo, add = low[some, col], [ref[some, col] for ref in digits]
                    for k in range(UNROLL):
                        hit = lo[k : k + 1] == place_in
                        carry = tuple(
                            total + jnp.where(hit, a[k : k + 1], 0)
                            for total, a in zip(carry, add)
                        )
                    return carry

                zero = (jnp.zeros((LOW, 128), I32),) * len(digits)
                totals = lax.fori_loop(0, SLOTS // UNROLL, step, zero)
                cl, place = q // 8, q % 8
                to = pl.ds(pl.multiple_of(place * 128, 128), 128)
                for b in range(CLUSTER // LOW):
                    count = ((totals[b // 4] >> (8 * (b % 4))) & 255).astype(F32)
                    self_at = place * 128 - b * LOW
                    count = count + jnp.where(place_in - lane == self_at, 2.0, 0.0)
                    a2t[cl, pl.ds(b * LOW, LOW), to] = count.astype(BF16)
                for at, kind, panel in COUNT_EVENTS:
                    pl.when(q == at)(lambda k=kind, p=panel: gather_event(k, p))

        pl.run_scoped(
            count_phase,
            pltpu.VMEM((nodes, SLOTS), I32),
            *[pltpu.VMEM((SLOTS, nodes), I32)] * (1 + CLUSTER // LOW // 4),
        )
        load_f.wait()

        @pl.loop(0, clusters * 2)
        def _(s):
            cl, j = s // 2, s % 2
            k = pl.ds(pl.multiple_of(cl * CLUSTER, CLUSTER), CLUSTER)
            col = pl.ds(pl.multiple_of(j * half_rows, half_rows), half_rows)
            total = dot(a2t[cl], fg[k, col], TN)
            scale = jnp.concatenate([fac[k, :]] * (half_rows // 128), axis=1)
            mixed[k, col] = (scale * total).astype(BF16)
            for at, kind, panel in MIX_EVENTS:
                pl.when(s == at)(lambda k=kind, p=panel: gather_event(k, p))

        def part(pt, t, **at):
            ys, xs = at.get("y", ALL), at.get("x", ALL)
            if t == "bias":
                zs = pl.ds(at["z"], 1) if "z" in at else ALL
                return ptb.at[ys, xs, c, zs]
            zs = pl.ds(pl.multiple_of(at["z"] * R, R), R) if "z" in at else ALL
            return pt.at[t // 2, ys, xs, zs, pl.ds(t % 2 * HC, HC)]

        def scatter_path(t):
            return SCATTER[0] if t == "bias" else SCATTER[t]

        def landing(t, k):
            return stage[(len(SCATTER) if t == "bias" else t) * 3 + k]

        def scatter_send(pt, t, k):
            path = scatter_path(t)

            def make(o):
                at = fixed(path[:k])
                at[path[k]] = me.shifted(path[k], o)
                return part(pt, t, **at), landing(t, k).at[o - 1], me.peer(path[k], o)

            for o in me.offsets(path[k]):
                send(("scatter", t, k, o), lambda o=o: make(o))

        def scatter_wait(t, k):
            for o in me.offsets(scatter_path(t)[k]):
                arrived(("scatter", t, k, o), landing(t, k).at[o - 1])

        def over_rows(shape, action):
            lead, high = shape[:-2], shape[-2]
            step = min(high, 64)

            def walk(index):
                if len(index) < len(lead):
                    if lead[len(index)] == 1:
                        walk(index + (0,))
                    else:
                        pl.loop(0, lead[len(index)])(lambda k: walk(index + (k,)))
                elif high == step:
                    action(index + (pl.ds(0, step),))
                else:
                    pl.loop(0, high // step)(
                        lambda k: action(
                            index + (pl.ds(pl.multiple_of(k * step, step), step),)
                        )
                    )

            walk(())

        def scatter_add(pt, t, k):
            path = scatter_path(t)
            mine = part(pt, t, **fixed(path[: k + 1]))
            others = [landing(t, k).at[o - 1] for o in me.offsets(path[k])]
            if t == "bias":
                total = mine[...]
                for other in others:
                    total = total + other[...]
                if k < 2:
                    mine[...] = total
                else:
                    gb_out[...] = total.reshape(8, 128)
                return

            def piece(at):
                total = mine[at].astype(F32)
                for other in others:
                    total = total + other[at].astype(F32)
                if k < 2:
                    mine[at] = total.astype(BF16)
                else:
                    gw_out[at[0], pl.ds(t * HC, HC)] = total

            over_rows(mine.shape, piece)

        def swap(po, j):
            i = sems["swap", 0] + j
            return pltpu.make_async_remote_copy(
                src_ref=po.at[j], dst_ref=cr.at[j],
                send_sem=ssem.at[i], recv_sem=rsem.at[i],
                device_id=me.peer("c", 1), device_id_type=MESH,
            )

        def scatter_event(pt, k, j):
            ts = (2 * j, 2 * j + 1) + (("bias",) if j == panels - 1 else ())
            for t in ts:
                scatter_wait(t, k - 1)
                scatter_add(pt, t, k - 1)
                if k < 3:
                    scatter_send(pt, t, k)

        def store_part(held, j, core, k):
            col = pl.ds(pl.multiple_of(j * PC, PC), PC)
            return pltpu.make_async_copy(
                held.at[j],
                gw_out.at[:, :, core, :, col],
                lsem.at[12 + (1 + k) * panels + j],
            )

        def panel_phase(pt, po, acc_a, acc_b, go, ac):
            def tile_rows(i):
                return pl.ds(pl.multiple_of(i * TM, TM), TM)

            def block(hbm, j, i):
                return hbm.at[tile_rows(i), pl.ds(pl.multiple_of(j * PC, PC), PC)]

            def load_g(j, i):
                return pltpu.make_async_copy(block(g_hbm, j, i), go.at[i], lsem.at[i])

            def store_act(j, i):
                return pltpu.make_async_copy(
                    ac.at[i], block(act_hbm, j, i), lsem.at[4 + i]
                )

            def product(j, i, cols):
                panel = wg[j, :, :, :, :, cols].reshape(width, GC)
                return dot(mixed[tile_rows(i), :], panel, NN)

            def finish(acc, j, i, cols):
                r = tile_rows(i)
                col = pl.ds(pl.multiple_of(j * PC + cols.start, GC), GC)
                v = acc[:, cols] + brow[0:1, col]
                u = v * v
                h = 0.5 + 0.5 * jnp.tanh(v * (ALPHA + BETA * u))
                a = v * h
                d = h + (a * (1.0 - h)) * (2 * ALPHA + (6 * BETA) * u)
                g = go[i, :, cols].astype(F32) * d
                ac[i, :, cols] = a.astype(BF16)
                fg[r, col] = g.astype(BF16)
                gbacc[:, col] += jnp.sum(g.reshape(TM // 8, 8, GC), axis=0)

            def weight_rows(j, core):
                lhs = [
                    mixed[:, pl.ds(pl.multiple_of((b * 2 + core) * SR, SR), SR)]
                    for b in range(Y * X)
                ]
                col = pl.ds(pl.multiple_of(j * PC, PC), PC)
                total = dot(jnp.concatenate(lhs, axis=1), fg[:, col], TN)
                return total.reshape(Y, X, SR, PC)

            def events(step):
                for at, kind, panel in PANEL_GATHER:
                    pl.when(step == at)(lambda k=kind, p=panel: gather_event(k, p))
                if not linked:
                    return
                for at, k, panel in PANEL_SCATTER:
                    pl.when(step == at)(lambda k=k, p=panel: scatter_event(pt, k, p))

            def send_bias():
                for d in range(n_dev):
                    col = pl.ds(d * R // 128 * 128, 128)
                    at = (d // (X * 2 * S), d // (2 * S) % X, d // S % 2, d % S)
                    ptb[at] = gbacc[:, col]
                send(
                    ("swap", "bias"),
                    lambda: (ptb.at[:, :, 1 - c], crb, me.peer("c", 1)),
                )

            def sum_bias():
                arrived(("swap", "bias"), crb)
                mine = ptb.at[:, :, c]
                mine[...] = mine[...] + crb[...]
                scatter_send(pt, "bias", 0)

            def pair(j, h):
                for k in range(2):
                    load_g(j, 2 * h + k).wait()
                    pl.when(j > 0)(lambda i=2 * h + k: store_act(j - 1, i).wait())
                for k, acc, other in ((0, acc_a, acc_b), (1, acc_b, acc_a)):
                    i = 2 * h + k
                    n = jnp.minimum(j * per_panel + i + 1, tiles - 1)
                    for q in range(PC // GC):
                        cols = pl.ds(q * GC, GC)
                        other[:, cols] = product(n // per_panel, n % per_panel, cols)
                        finish(acc, j, i, cols)
                for k in range(2):
                    i = 2 * h + k
                    store_act(j, i).start()
                    pl.when(j < panels - 1)(lambda i=i: load_g(j + 1, i).start())

            def own_rows(j):
                total = weight_rows(j, c)
                if linked:
                    swap(po, j).wait_recv()
                    total = total + cr[j].astype(F32)
                pt[j] = total.astype(BF16)
                if not linked:
                    store_part(pt, j, c, 0).start()
                    return
                for p in range(panels):

                    @pl.when(j == p)
                    def _():
                        for t in (2 * p, 2 * p + 1):
                            scatter_send(pt, t, 0)
                        if p == panels - 1:
                            sum_bias()

            def other_rows(j):
                po[j] = weight_rows(j, 1 - c).astype(BF16)
                if linked:
                    swap(po, j).start()
                    pl.when(j == panels - 1)(send_bias)
                else:
                    store_part(po, j, 1 - c, 1).start()

            def panel(j):
                @pl.loop(0, 2)
                def _(h):
                    pl.when(j < panels)(lambda: pair(j, h))
                    events(4 * j + 2 * h)
                    pl.when((h == 0) & (j > 0))(lambda: own_rows(j - 1))
                    pl.when((h == 1) & (j < panels))(lambda: other_rows(j))
                    events(4 * j + 2 * h + 1)

            for i in range(per_panel):
                load_g(0, i).start()
            gather_event("ready", 0)
            p = 128 // R
            if not linked:
                brow[...] = b_in[...]
            for k in range(width // 128 if linked else 0):
                tile = jnp.zeros((8, 128), F32)
                for d in range(k * p, (k + 1) * p):
                    tile = tile + bt[d // (X * 2 * S), d // (2 * S) % X, d // S % 2, d % S]
                brow[:, pl.ds(k * 128, 128)] = tile
            gbacc[...] = jnp.zeros_like(gbacc)
            for q in range(PC // GC):
                cols = pl.ds(q * GC, GC)
                acc_a[:, cols] = product(0, 0, cols)
            pl.loop(0, panels + 1)(panel)
            for i in range(per_panel):
                store_act(panels - 1, i).wait()

        def back_phase(pt, po):
            steps = nodes // BM

            @pl.loop(0, steps)
            def _(s):
                r = pl.ds(pl.multiple_of(s * BM, BM), BM)
                total = None
                for j in range(panels):
                    rhs = wg[j].reshape(width, PC)
                    term = dot(fg[r, pl.ds(j * PC, PC)], rhs, NT)
                    total = term if total is None else total + term
                scale = jnp.concatenate([fac[r, :]] * (width // 128), axis=1)
                fg[r, :] = (scale * total).astype(BF16)
                if not linked:
                    return

                for at, k, panel in BACK_SCATTER:
                    pl.when(s == at)(lambda k=k, p=panel: scatter_event(pt, k, p))

            if linked:
                scatter_event(pt, 3, panels - 1)
                for j in range(panels):
                    swap(po, j).wait_send()
                for name, make in started.items():
                    remote(name, *make()).wait_send()
            else:
                for j in range(panels):
                    store_part(pt, j, c, 0).wait()
                    store_part(po, j, 1 - c, 1).wait()
                gb_out[...] = gbacc[...]

        def with_parts(pt, po):
            pl.run_scoped(
                lambda *refs: panel_phase(pt, po, *refs),
                *[pltpu.VMEM((TM, PC), F32)] * 2,
                *[pltpu.VMEM((per_panel, TM, PC), BF16)] * 2,
            )
            back_phase(pt, po)

        pl.run_scoped(with_parts, *[pltpu.VMEM((panels, Y, X, SR, PC), BF16)] * 2)

    away = pl.BlockSpec(memory_space=pltpu.HBM)
    here = pl.BlockSpec(memory_space=pltpu.VMEM)
    scratch = [
        pltpu.VMEM((nodes, width), BF16),
        pltpu.VMEM((panels, Y, X, 2, SR, PC), BF16),
        pltpu.VMEM((nodes, 128), F32),
        pltpu.VMEM((8, 128), F32),
        pltpu.VMEM((Y, X, 2, S, 8, 128), F32),
        pltpu.VMEM((8, width), F32),
        pltpu.VMEM((8, width), F32),
        pltpu.VMEM((panels, Y, X, SR, PC), BF16),
        pltpu.VMEM((Y, X, S, 8, 128), F32),
        pltpu.VMEM((Y, X, 2, S, 8, 128), F32),
        *stage_shapes(),
        pltpu.SemaphoreType.DMA((n_sems,)),
        pltpu.SemaphoreType.DMA((n_sems,)),
        pltpu.SemaphoreType.DMA((12 + 3 * panels,)),
    ]
    if not linked:
        for k in (3, 4, 7, 8, 9, *range(10, 10 + n_stage)):
            scratch[k] = pltpu.VMEM((8, 128), F32)
        scratch[-3] = scratch[-2] = pltpu.SemaphoreType.DMA((1,))
    return pl.pallas_call(
        kernel,
        out_shape=(
            jax.ShapeDtypeStruct((nodes, width), BF16),
            pltpu.VMEM((nodes, width), BF16),
            pltpu.VMEM((clusters, CLUSTER, CLUSTER), BF16),
            pltpu.VMEM((R, width), F32)
            if linked
            else jax.ShapeDtypeStruct((Y, X, 2, SR, width), BF16),
            pltpu.VMEM((8, 128 if linked else width), F32),
        ),
        in_specs=[away] * 3 + [here, away],
        out_specs=(away, here, here, here if linked else away, here),
        scratch_shapes=scratch,
        compiler_params=pltpu.CompilerParams(
            collective_id=0 if linked else None,
            has_side_effects=True,
            vmem_limit_bytes=48 * 2**20,
        ),
        name="layer",
    )


def make_last(dp_size, shard_size, rows, width, nodes):
    clusters = nodes // CLUSTER
    per_cluster = width // PC
    steps = clusters * per_cluster
    part_rows = nodes // steps
    linked = linkable(rows)

    def kernel(links, spread, act_in, gw_in, gb_in, out, act_out, gw_out, gb_out, held, tiles, sem):
        def inward(k):
            part = act_in.at[pl.ds(pl.multiple_of(k * part_rows, part_rows), part_rows)]
            return pltpu.make_async_copy(part, held.at[k], sem.at[k])

        def outward(k):
            part = act_out.at[pl.ds(pl.multiple_of(k * part_rows, part_rows), part_rows)]
            return pltpu.make_async_copy(held.at[k], part, sem.at[steps + k])

        def place(k):
            return (
                pl.ds(pl.multiple_of(k // per_cluster * CLUSTER, CLUSTER), CLUSTER),
                pl.ds(pl.multiple_of(k % per_cluster * PC, PC), PC),
            )

        def store(k):
            return pltpu.make_async_copy(
                tiles.at[k % 2], out.at[place(k)], sem.at[2 * steps + k % 2]
            )

        carry = pltpu.make_async_copy(gw_in, gw_out, sem.at[2 * steps + 2])
        @pl.loop(0, steps)
        def _(k):
            inward(k).start()

        if linked:
            carry.start()
            me = Place(dp_size, shard_size)
            total = jnp.sum(gb_in[...], axis=0, keepdims=True)
            total = jnp.broadcast_to(total, (8, 128))
            gb_out[...] = pltpu.roll(total, (128 - me.lane(rows)) % 128, 1)[0:1, :rows]

        @pl.loop(0, steps)
        def _(k):
            pl.when(k >= 2)(lambda: store(k - 2).wait())
            tiles[k % 2] = dot(links[k // per_cluster], spread[place(k)], NN)
            store(k).start()
            inward(k).wait()
            outward(k).start()

        @pl.loop(0, steps)
        def _(k):
            outward(k).wait()

        for k in (steps - 2, steps - 1):
            store(k).wait()
        if linked:
            carry.wait()

    away = pl.BlockSpec(memory_space=pltpu.HBM)
    here = pl.BlockSpec(memory_space=pltpu.VMEM)
    return pl.pallas_call(
        kernel,
        out_shape=(
            jax.ShapeDtypeStruct((nodes, width), F32),
            jax.ShapeDtypeStruct((nodes, width), BF16),
            jax.ShapeDtypeStruct((rows, width), F32),
            jax.ShapeDtypeStruct((1, rows), F32),
        ),
        in_specs=[here, here, away, here, here],
        out_specs=(away, away, away, here),
        scratch_shapes=[
            pltpu.VMEM((steps, part_rows, width), BF16),
            pltpu.VMEM((2, CLUSTER, PC), F32),
            pltpu.SemaphoreType.DMA((2 * steps + 3,)),
        ],
        compiler_params=pltpu.CompilerParams(vmem_limit_bytes=14 * 2**20),
        name="features",
    )


def solution(mesh):
    dp_size, shard_size = mesh.shape["dp"], mesh.shape["shard"]

    def keep(array):
        return pltpu.with_memory_space_constraint(array, pltpu.VMEM)

    def leave(array):
        return pltpu.with_memory_space_constraint(array, pltpu.HBM)

    def on_device(features, neighbors, weight, bias_terms, grad_out):
        nodes, width = features.shape
        rows = weight.shape[0]
        layer = make_kernel(dp_size, shard_size, rows, width, nodes)
        last = make_last(dp_size, shard_size, rows, width, nodes)
        if linkable(rows):
            act, spread, links, grad_weight, bias_sums = layer(
                features, neighbors, weight, bias_terms.reshape(1, rows), grad_out
            )
            grad_features, output, grad_weight, grad_bias = last(
                keep(links), keep(spread), leave(act), keep(grad_weight), keep(bias_sums)
            )
            return output, grad_features, grad_weight, grad_bias.reshape(rows)
        both = ("dp", "shard")
        full = lax.all_gather(weight, both, axis=0, tiled=True)
        bias = lax.all_gather(bias_terms, both, axis=0, tiled=True).astype(F32)
        act, spread, links, parts, bias_sums = layer(
            features,
            neighbors,
            full.reshape(dp_size // 4, 2, 2, shard_size * rows, width),
            jnp.broadcast_to(bias, (8, width)),
            grad_out,
        )
        grad_features, output, *_ = last(
            keep(links),
            keep(spread),
            leave(act),
            jnp.zeros((rows, width), F32),
            jnp.zeros((8, 128), F32),
        )
        parts = parts.reshape(width, width).astype(F32)
        bias_sums = jnp.sum(bias_sums, axis=0)
        return (
            output,
            grad_features,
            lax.psum_scatter(parts, both, scatter_dimension=0, tiled=True),
            lax.psum_scatter(bias_sums, both, scatter_dimension=0, tiled=True),
        )

    split = P(("dp", "shard"), None)
    flat = P(("dp", "shard"))
    return jax.shard_map(
        on_device,
        mesh=mesh,
        in_specs=(split, split, split, flat, split),
        out_specs=(split, split, split, flat),
        check_vma=False,
    )
```
